32 devices in a mesh: gx: 16 (over z, y, x), gy: 2 (over core).
Axes of the slice: x: 2, y: 2, z: 4, core: 2. Of those that a mesh axis runs over, the one named last changes fastest.
Arguments:
- loads: bfloat16 [16, 2, 512, 128], P('gx', 'gy'), may hold values from -16 to 16
- schur: bfloat16 [16, 2, 512, 512], P('gx', 'gy'), may hold values from -0.5 to 3.5, as said below
- local_inverse: bfloat16 [16, 2, 512, 512], P('gx', 'gy'), may hold values from -0.5 to 3.5, as said below
- coarse_basis: float32 [16, 2, 4, 512], P('gx', 'gy'), may hold values from -0.75 to 0.75
- coarse_inverse: float32 [16, 2, 4, 128], P('gx', 'gy'), may hold values from -0.5 to 2, as said below
- face_map: int32 [16, 2, 512], P('gx', 'gy'), may hold values from 0 to 511, each once within a row
Outputs:
- solution: float32 [16, 2, 512, 128], P('gx', 'gy')
The draws below stay inside these ranges and needn't reach their ends.
Inputs may be any that keep to these rules, and one draw needn't show every extreme that they name: `face_map`: each subdomain's row is a permutation of its 512 interface slots. `schur`: each subdomain's matrix is symmetric and positive definite. `local_inverse`: each subdomain's matrix is symmetric and positive definite. `coarse_inverse`: the whole 128 x 128 matrix is symmetric and positive definite.
All inputs are finite; a program needn't handle non-finite values.
Results may differ from the reference program's by a relative error of at most 0.0006.
The reference program's roundings to bfloat16 on the way count: a program that leaves them out, or rounds other values in their place, can miss the bound.
Values sent between devices are 32-bit elements; how exact they have to be, the bound alone decides.
No kernel may reach another device: no remote copies, remote signals or barrier semaphores. Data moves between devices by JAX's collectives and lax.ppermute only.
A program may use at most 64 MiB of HBM per device.

```python
import math
import jax
import jax.numpy as jnp
from jax import lax

NI = 512
COLS = 128
NCO = 4
ITERS = 2
FACE = 128
SX = 16
SY = 2
NC = 128


def symmetric_block(subkey, matrix_order, lowest, highest, spread):
    first_key, second_key = jax.random.split(subkey)
    entries = jnp.clip(jax.random.normal(first_key, (matrix_order, matrix_order), jnp.float32), -4.0, 4.0)
    off_scale = spread / math.sqrt(matrix_order) / 1.4142135
    diagonal = jnp.exp(jax.random.uniform(second_key, (matrix_order,), jnp.float32, math.log(lowest), math.log(highest)))
    return (entries + entries.T) * off_scale + jnp.diag(diagonal)


def subdomain_matrices(key, salt_value, lowest, highest):
    keys_all = jax.random.split(jax.random.fold_in(key, salt_value), SX * SY)

    def single(subkey):
        return symmetric_block(subkey, NI, lowest, highest, 0.6)
    return lax.map(single, keys_all).reshape(SX, SY, NI, NI).astype(jnp.bfloat16)


def draw_schur(key, part):
    return subdomain_matrices(key, 11, 1.5, 3.0)


def draw_local_inverse(key, part):
    return subdomain_matrices(key, 23, 1.5, 3.0)


def draw_coarse_inverse(key, part):
    full_matrix = symmetric_block(jax.random.fold_in(key, 37), NC, 1.0, 1.6, 0.4)
    return full_matrix.reshape(SX, SY, NCO, NC).astype(jnp.float32)


def draw_loads(key, part):
    first_key = jax.random.fold_in(jax.random.fold_in(key, 41), 0)
    ramp_scale = 1.0 + 2.0 * jnp.arange(SX * SY, dtype=jnp.float32) / (SX * SY - 1)
    entries = jnp.clip(jax.random.normal(first_key, (SX * SY, NI, COLS), jnp.float32), -5.0, 5.0)
    return (entries * ramp_scale[:, None, None]).reshape(SX, SY, NI, COLS).astype(jnp.bfloat16)


def block_levels(rng, shape, shards, low, largest):
    def one(axis_at, blocks):
        draws = jax.random.uniform(jax.random.fold_in(jax.random.fold_in(rng, 6), axis_at), (blocks,), jnp.float32, low / len(shards), largest / len(shards))
        return jnp.repeat(jnp.exp(draws), shape[axis_at] // blocks).reshape((-1,) + (1,) * (len(shape) - axis_at - 1))

    factor_of = one(*shards[0])
    for cut in shards[1:]:
        factor_of = factor_of * one(*cut)
    return factor_of


def centred(stream_key, extent, width, most, cuts=(), kind=jnp.bfloat16):
    result = width * jax.random.normal(stream_key, extent, jnp.float32)
    if cuts:
        result = result * block_levels(stream_key, extent, cuts, -0.22, 0.18)
    return jnp.clip(result, -most, most).astype(kind)


def setup_inputs(seed: int = 0) -> dict:
    streams_of = jax.random.split(jax.random.key(seed), 7)
    loads = draw_loads(jax.random.fold_in(streams_of[6], 71), 0)
    schur = draw_schur(jax.random.fold_in(streams_of[6], 71), 0)
    local_inverse = draw_local_inverse(jax.random.fold_in(streams_of[6], 71), 0)
    coarse_basis = centred(streams_of[3], (SX, SY, NCO, NI), 64 ** -0.5, 0.75, ((0, 16), (1, 2)), jnp.float32)
    coarse_inverse = draw_coarse_inverse(jax.random.fold_in(streams_of[6], 71), 0)
    face_map = jax.vmap(lambda own: jax.random.permutation(own, NI))(jax.random.split(streams_of[5], SX * SY)).reshape((SX, SY, NI)).astype(jnp.int32)
    return dict(loads=loads, schur=schur, local_inverse=local_inverse, coarse_basis=coarse_basis, coarse_inverse=coarse_inverse, face_map=face_map)


def face_weights():
    lower_x = jnp.where(jnp.arange(SX) > 0, 0.5, 1.0)
    upper_x = jnp.where(jnp.arange(SX) < SX - 1, 0.5, 1.0)
    lower_y = jnp.where(jnp.arange(SY) > 0, 0.5, 1.0)
    upper_y = jnp.where(jnp.arange(SY) < SY - 1, 0.5, 1.0)
    shape_face = (SX, SY, FACE, 1)
    pieces = [jnp.broadcast_to(lower_x[:, None, None, None], shape_face), jnp.broadcast_to(upper_x[:, None, None, None], shape_face), jnp.broadcast_to(lower_y[None, :, None, None], shape_face), jnp.broadcast_to(upper_y[None, :, None, None], shape_face)]
    return jnp.concatenate(pieces, axis=2).astype(jnp.float32)

def assemble(values):
    west_face = values[:, :, 0:FACE]
    east_face = values[:, :, FACE:2 * FACE]
    south_face = values[:, :, 2 * FACE:3 * FACE]
    north_face = values[:, :, 3 * FACE:]
    blank_x = jnp.zeros_like(west_face[:1])
    blank_y = jnp.zeros_like(south_face[:, :1])
    west_sum = west_face + jnp.concatenate([blank_x, east_face[:-1]], axis=0)
    east_sum = east_face + jnp.concatenate([west_face[1:], blank_x], axis=0)
    south_sum = south_face + jnp.concatenate([blank_y, north_face[:, :-1]], axis=1)
    north_sum = north_face + jnp.concatenate([south_face[:, 1:], blank_y], axis=1)
    return jnp.concatenate([west_sum, east_sum, south_sum, north_sum], axis=2)

def permuted_product(matrices, halves, face_map):

    def single(operands):
        matrix, column_block, index_map = operands
        gathered = column_block[index_map]
        product = jnp.dot(matrix.astype(jnp.float32), gathered.astype(jnp.float32), precision=lax.Precision.HIGHEST, preferred_element_type=jnp.float32)
        return jnp.zeros_like(product).at[index_map].set(product)
    outputs = lax.map(single, (matrices.reshape(SX * SY, NI, NI), halves.reshape(SX * SY, NI, COLS), face_map.reshape(SX * SY, NI)))
    return outputs.reshape(SX, SY, NI, COLS)

def gram(left_mat, right_mat):
    return jnp.einsum('abik,abil->kl', left_mat.astype(jnp.float32), right_mat.astype(jnp.float32), precision=lax.Precision.HIGHEST, preferred_element_type=jnp.float32)

def solve_gram(matrix, right_side):
    factor = jnp.linalg.cholesky(matrix)
    return jax.scipy.linalg.cho_solve((factor, True), right_side)

def times_small(values, small_matrix):
    return jnp.einsum('abik,kl->abil', values.astype(jnp.float32), small_matrix.astype(jnp.float32), precision=lax.Precision.HIGHEST, preferred_element_type=jnp.float32)

def precondition(residual, weights, local_inverse, coarse_basis, coarse_inverse, face_map):
    scaled = weights * residual
    local_part = permuted_product(local_inverse, scaled.astype(jnp.bfloat16), face_map)
    coarse_input = jnp.einsum('abcn,abnk->abck', coarse_basis.astype(jnp.float32), scaled.astype(jnp.float32), precision=lax.Precision.HIGHEST, preferred_element_type=jnp.float32)
    coarse_values = jnp.dot(coarse_inverse.reshape(NC, NC).astype(jnp.float32), coarse_input.reshape(NC, COLS).astype(jnp.float32), precision=lax.Precision.HIGHEST, preferred_element_type=jnp.float32)
    coarse_values = coarse_values.reshape(SX, SY, NCO, COLS)
    correction = local_part + jnp.einsum('abcn,abck->abnk', coarse_basis.astype(jnp.float32), coarse_values.astype(jnp.float32), precision=lax.Precision.HIGHEST, preferred_element_type=jnp.float32)
    return assemble(weights * correction)

def reference(loads, schur, local_inverse, coarse_basis, coarse_inverse, face_map):
    weights = face_weights()
    residual = assemble(loads.astype(jnp.float32))
    solution = jnp.zeros_like(residual)
    update = precondition(residual, weights, local_inverse, coarse_basis, coarse_inverse, face_map)
    precond_gram = gram(residual, weights * update)
    direction = update
    for iteration in range(ITERS):
        image_vec = assemble(permuted_product(schur, direction.astype(jnp.bfloat16), face_map))
        curvature = gram(direction, weights * image_vec)
        step_size = solve_gram(curvature, precond_gram)
        solution = solution + times_small(direction, step_size)
        if iteration + 1 < ITERS:
            residual = residual - times_small(image_vec, step_size)
            update = precondition(residual, weights, local_inverse, coarse_basis, coarse_inverse, face_map)
            next_gram = gram(residual, weights * update)
            ratio_coef = solve_gram(precond_gram, next_gram)
            direction = update + times_small(direction, ratio_coef)
            precond_gram = next_gram
    return solution
```

```python
import functools

import jax
import jax.numpy as jnp
from jax import lax
from jax.experimental import pallas as pl
from jax.experimental.pallas import tpu as pltpu
from jax.sharding import PartitionSpec as P

AXES = ("gx", "gy")
F32 = jnp.float32
BF16 = jnp.bfloat16
EXACT = lax.Precision.HIGHEST


def dot(left, right, left_dim=1, right_dim=0, precision=EXACT):
    return lax.dot_general(
        left,
        right,
        (((left_dim,), (right_dim,)), ((), ())),
        precision=precision,
        preferred_element_type=F32,
    )


def half_dot(left, right):
    return lax.dot_general(
        left, right, (((1,), (0,)), ((), ())), preferred_element_type=F32
    )


def call(body, outs, scratch=(), flops=0, moved=0):
    return pl.pallas_call(
        body,
        scratch_shapes=[pltpu.VMEM(shape, kind) for shape, kind in scratch],
        out_shape=[jax.ShapeDtypeStruct(shape, kind) for shape, kind in outs],
        compiler_params=pltpu.CompilerParams(vmem_limit_bytes=48 * 1024 * 1024),
        cost_estimate=pl.CostEstimate(flops=flops, bytes_accessed=moved, transcendentals=0),
    )


def pair_rounds(size):
    first = [(i, i + 1) for i in range(0, size - 1, 2)]
    second = [(i, i + 1) for i in range(1, size - 1, 2)]
    return [pairs + [(j, i) for i, j in pairs] for pairs in (first, second)]


def exchange(sends):
    got = []
    for axis, pieces in zip(AXES, (sends[0:2], sends[2:4])):
        for pairs, piece in zip(pair_rounds(lax.axis_size(axis)), pieces):
            got.append(lax.ppermute(piece, axis, pairs) if pairs else None)
    return got


def rounds_used():
    return [bool(p) for axis in AXES for p in pair_rounds(lax.axis_size(axis))]


def even(axis):
    return lax.rem(lax.axis_index(axis), 2) == 0


def to_rounds(faces):
    ex, ey = even("gx"), even("gy")
    return [
        jnp.where(ex, faces[1], faces[0]),
        jnp.where(ex, faces[0], faces[1]),
        jnp.where(ey, faces[3], faces[2]),
        jnp.where(ey, faces[2], faces[3]),
    ]


def to_faces(parts):
    ex, ey = even("gx"), even("gy")
    a, b, c, d = parts

    def choose(flag, yes, no):
        if yes is None and no is None:
            return None
        if yes is None:
            return jnp.where(flag, jnp.zeros_like(no), no)
        if no is None:
            return jnp.where(flag, yes, jnp.zeros_like(yes))
        return jnp.where(flag, yes, no)

    return [choose(ex, b, a), choose(ex, a, b), choose(ey, d, c), choose(ey, c, d)]


def face_weights():
    ix, iy = lax.axis_index("gx"), lax.axis_index("gy")
    shared = [
        ix > 0,
        ix < lax.axis_size("gx") - 1,
        iy > 0,
        iy < lax.axis_size("gy") - 1,
    ]
    return [jnp.where(flag, 0.5, 1.0).astype(F32) for flag in shared]


def split_faces(field):
    rows = field.shape[0] // 4
    return [field[rows * f : rows * (f + 1)] for f in range(4)]


def add_faces(field, got):
    faces = [
        mine if other is None else mine + other for mine, other in zip(split_faces(field), got)
    ]
    return jnp.concatenate(faces, axis=0)


def weighted(field, weights):
    return jnp.concatenate([w * v for w, v in zip(weights, split_faces(field))], axis=0)


def write_blocks(out_ref, rows):
    out_ref[...] = jnp.zeros(out_ref.shape, F32)
    per = out_ref.shape[1]
    used = rows.shape[0] // per
    out_ref[0:used] = rows.reshape(used, per, rows.shape[1])


def unit_inverse(matrix, work_ref):
    size = matrix.shape[0]
    row_id = lax.broadcasted_iota(jnp.int32, (size, size), 0)
    col_id = lax.broadcasted_iota(jnp.int32, (size, size), 1)
    eye = (row_id == col_id).astype(F32)
    only = matrix * eye
    by_row = lax.rsqrt(jnp.sum(only, axis=1, keepdims=True))
    by_col = lax.rsqrt(jnp.sum(only, axis=0, keepdims=True))
    unit = matrix * by_row * by_col
    bound = jnp.max(jnp.sum(jnp.abs(unit), axis=0, keepdims=True), axis=1, keepdims=True)
    scale = 2.0 / (1.0 + bound)
    power = eye - scale * unit
    total = eye + power
    power = dot(power, power)

    def step(total, power):
        both = dot(jnp.concatenate([total, power], axis=0), power)
        return total + both[:size], both[size:]

    for _ in range(3):
        total, power = step(total, power)
    work_ref[0:size] = total
    work_ref[size:] = power

    def again(carry):
        total, power = step(work_ref[0:size], work_ref[size:])
        work_ref[0:size] = total
        work_ref[size:] = power
        return carry[0] + 1, jnp.max(jnp.abs(power))

    lax.while_loop(
        lambda carry: jnp.logical_and(carry[0] < 40, carry[1] > 1e-7),
        again,
        (jnp.int32(0), jnp.max(jnp.abs(power))),
    )
    return work_ref[0:size] * (by_row * scale) * by_col


def local(loads, schur, local_inverse, coarse_basis, coarse_inverse, face_map):
    loads, schur, local_inverse = loads[0, 0], schur[0, 0], local_inverse[0, 0]
    basis, coarse_rows, slot_map = coarse_basis[0, 0], coarse_inverse[0, 0], face_map[0, 0]
    unknowns, cols = loads.shape
    face = unknowns // 4
    nco, coarse_all = coarse_rows.shape
    devices = lax.axis_size("gx") * lax.axis_size("gy")
    chunks = coarse_all // cols
    used = rounds_used()
    field = (unknowns, cols)
    gram_shape = (cols, cols)
    work = [((2 * cols, cols), F32)]
    face_out = ((face, cols), F32)

    def give(refs, faces):
        for ref, value, flag in zip(refs, to_rounds(faces), used):
            if flag:
                ref[...] = value

    def take(refs):
        return to_faces([ref[...] if flag else None for ref, flag in zip(refs, used)])

    def trade(sends):
        return [got for got in exchange(sends) if got is not None]

    def spread(refs):
        left = list(refs)
        return [left.pop(0) if flag else None for flag in used]

    nrounds = sum(used)

    def fill(values):
        left = list(values)
        return [left.pop(0) if flag else None for flag in used]

    head = face + nco + nco * chunks

    def send_loads(loads_ref, basis_ref, rows_ref, *outs):
        outs = spread(outs)
        basis_now = basis_ref[...]
        rows_now = rows_ref[...]
        packs = []
        for f, part in enumerate(split_faces(loads_ref[...].astype(F32))):
            packs.append(
                jnp.concatenate(
                    [part, basis_now[:, face * f : face * (f + 1)]]
                    + [rows_now[:, cols * c : cols * (c + 1)] for c in range(chunks)],
                    axis=0,
                )
            )
        give(outs, packs)

    sends = call(send_loads, [((head, cols), F32)] * nrounds)(loads, basis, coarse_rows)
    got_a = trade(fill(sends))

    def reorder(map_ref, first_ref, second_ref, first_out, second_out):
        slots = lax.broadcasted_iota(jnp.int32, (unknowns, unknowns), 0)
        pick = (slots == map_ref[...]).astype(F32).astype(BF16)
        for ref, out in ((first_ref, first_out), (second_ref, second_out)):
            rows = half_dot(pick, ref[...]).astype(BF16)
            out[...] = lax.dot_general(
                rows, pick, (((1,), (1,)), ((), ())), preferred_element_type=F32
            ).astype(BF16)

    inverse_here, schur_here = call(
        reorder, [((unknowns, unknowns), BF16)] * 2, flops=8 * unknowns**3, moved=8 * unknowns**2
    )(slot_map.reshape(1, unknowns), local_inverse, schur)

    def first_local(*refs):
        got = take(spread(refs[:nrounds]))
        loads_ref, inverse_ref, basis_ref, rows_ref = refs[nrounds : nrounds + 4]
        res_ref, part_ref, gram_ref, ci_ref, bases_ref, table_ref = refs[nrounds + 4 : nrounds + 10]
        sends = spread(refs[nrounds + 10 :])
        weights = face_weights()
        residual = add_faces(loads_ref[...].astype(F32), [g if g is None else g[:face] for g in got])
        scaled = weighted(residual, weights)
        product = half_dot(inverse_ref[...], scaled.astype(BF16))
        part = weighted(product, weights)
        give(sends, split_faces(part))
        res_ref[...] = residual
        part_ref[...] = part
        gram_ref[...] = dot(scaled, product, 0, 0)
        coarse_input = dot(basis_ref[...], scaled)
        ci_ref[...] = jnp.broadcast_to(coarse_input[None], ci_ref.shape)
        basis_now = basis_ref[...]
        bases, tables = [], []
        for f in range(4):
            mine = weights[f] * basis_now[:, face * f : face * (f + 1)]
            other = got[f]
            if other is None:
                bases += [mine, jnp.zeros_like(mine)]
                tables += [rows_ref[...], jnp.zeros((nco, coarse_all), F32)]
            else:
                bases += [mine, 0.5 * other[face : face + nco]]
                tables += [
                    rows_ref[...],
                    jnp.concatenate(
                        [
                            other[face + nco * (c + 1) : face + nco * (c + 2)]
                            for c in range(chunks)
                        ],
                        axis=1,
                    ),
                ]
        bases_ref[...] = jnp.concatenate(bases, axis=0)
        table_ref[...] = jnp.concatenate(tables, axis=0)

    outs = call(
        first_local,
        [
            (field, F32),
            (field, F32),
            (gram_shape, F32),
            ((devices, nco, cols), F32),
            ((8 * nco, face), F32),
            ((8 * nco, coarse_all), F32),
        ]
        + [face_out] * nrounds,
    )(*got_a, loads, inverse_here, basis, coarse_rows)
    residual, part, gram_part, coarse_input, bases, table = outs[:6]
    got_b = trade(fill(outs[6:]))
    coarse_all_in = lax.all_to_all(coarse_input, AXES, 0, 0).reshape(coarse_all, cols)

    def coarse_part(bases_now, values):
        return [
            dot(bases_now[2 * nco * f : 2 * nco * (f + 1)], values[2 * nco * f : 2 * nco * (f + 1)], 0, 0)
            for f in range(4)
        ]

    per = 8 * -(-2 * cols // (8 * devices))

    def first_direction(*refs):
        got = take(spread(refs[:nrounds]))
        part_ref, gram_ref, all_ref, bases_ref, table_ref, schur_ref, mine_ref = refs[
            nrounds : nrounds + 7
        ]
        dir_ref, image_ref, values_ref, blocks_ref = refs[nrounds + 7 : nrounds + 11]
        sends = spread(refs[nrounds + 11 :])
        values = dot(table_ref[...], all_ref[...])
        values_ref[...] = values
        coarse = coarse_part(bases_ref[...], values)
        update = add_faces(part_ref[...], got) + jnp.concatenate(coarse, axis=0)
        dir_ref[...] = update
        image = half_dot(schur_ref[...], update.astype(BF16))
        image_ref[...] = image
        give(sends, split_faces(image))
        first = gram_ref[...] + dot(mine_ref[0], values[:nco], 0, 0)
        curvature = dot(update, image, 0, 0)
        write_blocks(blocks_ref, jnp.concatenate([curvature, first], axis=0))

    outs = call(
        first_direction,
        [
            (field, F32),
            (field, F32),
            ((8 * nco, cols), F32),
            ((devices, per, cols), F32),
        ]
        + [face_out] * nrounds,
    )(*got_b, part, gram_part, coarse_all_in, bases, table, schur_here, coarse_input)
    direction, image, values, blocks = outs[:4]
    got_d = trade(fill(outs[4:]))
    blocks = lax.all_to_all(blocks, AXES, 0, 0)

    def first_sums(*refs):
        got = take(spread(refs[:nrounds]))
        image_ref, blocks_ref, basis_ref = refs[nrounds : nrounds + 3]
        full_ref, sum_ref, mine_ref = refs[nrounds + 3 :]
        image_vec = add_faces(image_ref[...], got)
        full_ref[...] = image_vec
        coarse_image = dot(basis_ref[...], weighted(image_vec, face_weights()))
        mine_ref[...] = coarse_image
        block = jnp.concatenate(
            [jnp.sum(blocks_ref[...], axis=0), coarse_image, jnp.zeros((8 - nco, cols), F32)], axis=0
        )
        sum_ref[...] = jnp.broadcast_to(block[None], sum_ref.shape)

    image_vec, sums, coarse_image = call(
        first_sums,
        [(field, F32), ((devices, per + 8, cols), F32), ((nco, cols), F32)],
    )(*got_d, image, blocks, basis)
    sums = lax.all_to_all(sums, AXES, 0, 0)

    def second_local(
        sums_ref, res_ref, full_ref, inverse_ref, table_ref, values_ref, mine_ref, image_ref, *outs
    ):
        outs, work_ref = outs[:-1], outs[-1]
        curv_ref, first_ref, step_ref, next_ref, values_out, part_ref = outs[:6]
        sends = spread(outs[6:])
        both = sums_ref[:, 0:per, :].reshape(devices * per, cols)
        curvature, first = both[:cols], both[cols : 2 * cols]
        step = dot(unit_inverse(curvature, work_ref), first)
        weights = face_weights()
        residual = res_ref[...] - dot(full_ref[...], step)
        scaled = weighted(residual, weights)
        product = half_dot(inverse_ref[...], scaled.astype(BF16))
        part = weighted(product, weights)
        part_ref[...] = part
        give(sends, split_faces(part))
        curv_ref[...] = curvature
        first_ref[...] = first
        step_ref[...] = step
        wide = cols // nco * 8
        src = lax.broadcasted_iota(jnp.int32, (cols, wide), 0)
        dst = lax.broadcasted_iota(jnp.int32, (cols, wide), 1)
        widen = (dst == src // nco * 8 + lax.rem(src, nco)).astype(F32)
        rows = sums_ref[:, per : per + 8, :].reshape(devices * 8, cols)
        got = values_ref[...] * 0.0
        for c in range(chunks):
            table_c = dot(table_ref[:, cols * c : cols * (c + 1)], widen)
            got = got + dot(table_c, rows[wide * c : wide * (c + 1)])
        values_now = values_ref[...] - dot(got, step)
        values_out[...] = values_now
        own = mine_ref[0] - dot(image_ref[...], step)
        next_ref[...] = dot(scaled, product, 0, 0) + dot(own, values_now[:nco], 0, 0)

    outs = call(
        second_local,
        [
            (gram_shape, F32),
            (gram_shape, F32),
            (gram_shape, F32),
            (gram_shape, F32),
            ((8 * nco, cols), F32),
            (field, F32),
        ]
        + [face_out] * nrounds,
        work,
    )(sums, residual, image_vec, inverse_here, table, values, coarse_input, coarse_image)
    curvature, first, step, next_part, values, part = outs[:6]
    got_e = trade(fill(outs[6:]))

    def invert(first_ref, out_ref, work_ref):
        out_ref[...] = unit_inverse(first_ref[...], work_ref)

    (first_inverse,) = call(invert, [(gram_shape, F32)], work, flops=2 * 60 * cols**3)(first)

    per2 = 8 * -(-3 * cols // (8 * devices))
    per2 = per2 if (3 * cols) % per2 == 0 else 8 * -(-4 * cols // (8 * devices))

    def second_direction(*refs):
        got = take(spread(refs[:nrounds]))
        part_ref, next_ref, values_ref, bases_ref, schur_ref, image_ref = refs[nrounds : nrounds + 6]
        update_ref, blocks_ref = refs[nrounds + 6 :]
        coarse = coarse_part(bases_ref[...], values_ref[...])
        update = add_faces(part_ref[...], got) + jnp.concatenate(coarse, axis=0)
        update_ref[...] = update
        product = half_dot(schur_ref[...], update.astype(BF16))
        square = dot(update, product, 0, 0)
        cross = dot(image_ref[...], update, 0, 0)
        rows = [next_ref[...], square, cross]
        if (3 * cols) % per2:
            rows.append(jnp.zeros(gram_shape, F32))
        write_blocks(blocks_ref, jnp.concatenate(rows, axis=0))

    update, blocks = call(
        second_direction, [(field, F32), ((devices, per2, cols), F32)]
    )(*got_e, part, next_part, values, bases, schur_here, image)
    blocks = lax.all_to_all(blocks, AXES, 0, 0)

    def second_sums(blocks_ref, out_ref):
        out_ref[...] = jnp.broadcast_to(jnp.sum(blocks_ref[...], axis=0)[None], out_ref.shape)

    (sums,) = call(second_sums, [((devices, per2, cols), F32)])(blocks)
    sums = lax.all_to_all(sums, AXES, 0, 0).reshape(devices * per2, cols)

    def finish(sums_ref, first_ref, curv_ref, step_ref, dir_ref, update_ref, out_ref, work_ref):
        rows = sums_ref[...]
        next_gram, square, cross = (rows[cols * k : cols * (k + 1)] for k in range(3))
        ratio = dot(first_ref[...], next_gram)
        mixed = dot(cross, ratio, 0, 0)
        curvature = square + mixed + mixed.T + dot(ratio, dot(curv_ref[...], ratio), 0, 0)
        step = dot(unit_inverse(curvature, work_ref), next_gram)
        total = step_ref[...] + dot(ratio, step)
        out_ref[...] = dot(dir_ref[...], total) + dot(update_ref[...], step)

    (solved,) = call(finish, [(field, F32)], work)(
        sums, first_inverse, curvature, step, direction, update
    )
    return solved[None, None]


def solution(mesh):
    return jax.shard_map(
        local,
        mesh=mesh,
        in_specs=(
            P("gx", "gy", None, None),
            P("gx", "gy", None, None),
            P("gx", "gy", None, None),
            P("gx", "gy", None, None),
            P("gx", "gy", None, None),
            P("gx", "gy", None),
        ),
        out_specs=P("gx", "gy", None, None),
        check_vma=False,
    )
```

```python
import jax
import jax.numpy as jnp
from jax import lax
from jax.experimental import pallas as pl
from jax.experimental.pallas import tpu as pltpu
from jax.sharding import PartitionSpec as P

AXES = ("gx", "gy")
F32 = jnp.float32
BF16 = jnp.bfloat16
EXACT = lax.Precision.HIGHEST


def dot(left, right, left_dim=1, right_dim=0, precision=EXACT):
    return lax.dot_general(
        left,
        right,
        (((left_dim,), (right_dim,)), ((), ())),
        precision=precision,
        preferred_element_type=F32,
    )


def half_dot(left, right):
    return lax.dot_general(
        left, right, (((1,), (0,)), ((), ())), preferred_element_type=F32
    )


def call(body, outs, scratch=(), flops=0, moved=0, far=0, copies=0):
    sems = [pltpu.SemaphoreType.DMA((copies,))] if copies else []

    def run(*args):
        specs = [pl.BlockSpec(memory_space=pltpu.HBM if i < far else pltpu.VMEM) for i in range(len(args))]
        args = [pltpu.with_memory_space_constraint(a, pltpu.HBM) if i < far else a for i, a in enumerate(args)]
        return kernel_call(body, outs, scratch, flops, moved, sems, specs)(*args)

    return run


def kernel_call(body, outs, scratch, flops, moved, sems, specs):
    return pl.pallas_call(
        body,
        in_specs=specs,
        scratch_shapes=[pltpu.VMEM(shape, kind) for shape, kind in scratch] + sems,
        out_shape=[jax.ShapeDtypeStruct(shape, kind) for shape, kind in outs],
        compiler_params=pltpu.CompilerParams(vmem_limit_bytes=48 * 1024 * 1024),
        cost_estimate=pl.CostEstimate(flops=flops, bytes_accessed=moved, transcendentals=0),
    )


def pair_rounds(size):
    first = [(i, i + 1) for i in range(0, size - 1, 2)]
    second = [(i, i + 1) for i in range(1, size - 1, 2)]
    return [pairs + [(j, i) for i, j in pairs] for pairs in (first, second)]


def exchange(sends):
    got = []
    for axis, pieces in zip(AXES, (sends[0:2], sends[2:4])):
        for pairs, piece in zip(pair_rounds(lax.axis_size(axis)), pieces):
            got.append(lax.ppermute(piece, axis, pairs) if pairs else None)
    return got


def rounds_used():
    return [bool(p) for axis in AXES for p in pair_rounds(lax.axis_size(axis))]


def even(axis):
    return lax.rem(lax.axis_index(axis), 2) == 0


def to_rounds(faces):
    ex, ey = even("gx"), even("gy")
    return [
        jnp.where(ex, faces[1], faces[0]),
        jnp.where(ex, faces[0], faces[1]),
        jnp.where(ey, faces[3], faces[2]),
        jnp.where(ey, faces[2], faces[3]),
    ]


def to_faces(parts):
    ex, ey = even("gx"), even("gy")
    a, b, c, d = parts

    def choose(flag, yes, no):
        if yes is None and no is None:
            return None
        if yes is None:
            return jnp.where(flag, jnp.zeros_like(no), no)
        if no is None:
            return jnp.where(flag, yes, jnp.zeros_like(yes))
        return jnp.where(flag, yes, no)

    return [choose(ex, b, a), choose(ex, a, b), choose(ey, d, c), choose(ey, c, d)]


def face_weights():
    ix, iy = lax.axis_index("gx"), lax.axis_index("gy")
    shared = [
        ix > 0,
        ix < lax.axis_size("gx") - 1,
        iy > 0,
        iy < lax.axis_size("gy") - 1,
    ]
    return [jnp.where(flag, 0.5, 1.0).astype(F32) for flag in shared]


def split_faces(field):
    rows = field.shape[0] // 4
    return [field[rows * f : rows * (f + 1)] for f in range(4)]


def add_faces(field, got):
    faces = [
        mine if other is None else mine + other for mine, other in zip(split_faces(field), got)
    ]
    return jnp.concatenate(faces, axis=0)


def weighted(field, weights):
    return jnp.concatenate([w * v for w, v in zip(weights, split_faces(field))], axis=0)


def write_blocks(out_ref, rows):
    per = out_ref.shape[1]
    used = rows.shape[0] // per
    if used < out_ref.shape[0]:
        out_ref[...] = jnp.zeros(out_ref.shape, F32)
    out_ref[0:used] = rows.reshape(used, per, rows.shape[1])


def solve(matrix, right, work_ref, boosts, squarings):
    size = matrix.shape[0]
    row_id = lax.broadcasted_iota(jnp.int32, (size, size), 0)
    col_id = lax.broadcasted_iota(jnp.int32, (size, size), 1)
    eye = (row_id == col_id).astype(F32)
    matrix = 0.5 * (matrix + matrix.T)
    only = matrix * eye
    by_row = lax.rsqrt(jnp.sum(only, axis=1, keepdims=True))
    by_col = lax.rsqrt(jnp.sum(only, axis=0, keepdims=True))
    unit = matrix * by_row * by_col
    bound = jnp.max(jnp.sum(jnp.abs(unit), axis=0, keepdims=True), axis=1, keepdims=True)
    scale = 1.9 / bound
    answer = right * (by_row * scale)
    power = eye - scale * unit

    def step(answer, power):
        both = dot(power, jnp.concatenate([answer, power], axis=1))
        return answer + both[:, :size], both[:, size:]

    for k in range(squarings):
        answer, power = step(answer, power)
        if k < len(boosts):
            power = boosts[k] * power + (1.0 - boosts[k]) * eye
            answer = boosts[k] * answer
    work_ref[:, 0:size] = answer + dot(power, answer)
    largest = jnp.max(jnp.abs(power))

    @pl.when(jnp.logical_not(largest < 3e-4))
    def _():
        work_ref[:, 0:size] = answer
        work_ref[:, size:] = power

        def again(carry):
            answer, power = step(work_ref[:, 0:size], work_ref[:, size:])
            work_ref[:, 0:size] = answer
            work_ref[:, size:] = power
            return carry[0] + 1, jnp.max(jnp.abs(power))

        lax.while_loop(
            lambda carry: jnp.logical_and(carry[0] < 40, carry[1] > 1e-7),
            again,
            (jnp.int32(0), largest),
        )

    return work_ref[:, 0:size] * by_row


def local(loads, schur, local_inverse, coarse_basis, coarse_inverse, face_map):
    loads, schur, local_inverse = loads[0, 0], schur[0, 0], local_inverse[0, 0]
    basis, coarse_rows, slot_map = coarse_basis[0, 0], coarse_inverse[0, 0], face_map[0, 0]
    unknowns, cols = loads.shape
    face = unknowns // 4
    nco, coarse_all = coarse_rows.shape
    devices = lax.axis_size("gx") * lax.axis_size("gy")
    chunks = coarse_all // cols
    used = rounds_used()
    field = (unknowns, cols)
    gram_shape = (cols, cols)
    work = [((cols, 2 * cols), F32)]
    face_out = ((face, cols), F32)

    def give(refs, faces):
        for ref, value, flag in zip(refs, to_rounds(faces), used):
            if flag:
                ref[...] = value

    def take(refs):
        return to_faces([ref[...] if flag else None for ref, flag in zip(refs, used)])

    def trade(sends):
        return [got for got in exchange(sends) if got is not None]

    def spread(refs):
        left = list(refs)
        return [left.pop(0) if flag else None for flag in used]

    nrounds = sum(used)

    def fill(values):
        left = list(values)
        return [left.pop(0) if flag else None for flag in used]

    head = face + nco + nco * chunks

    def send_loads(loads_hbm, basis_hbm, rows_hbm, loads_ref, basis_ref, rows_ref, *outs):
        outs, raw_ref, sems = spread(outs[:-2]), outs[-2], outs[-1]
        fetches = [
            pltpu.make_async_copy(src, dst, sems.at[k])
            for k, (src, dst) in enumerate(
                ((loads_hbm, raw_ref), (basis_hbm, basis_ref), (rows_hbm, rows_ref))
            )
        ]
        for fetch in fetches:
            fetch.start()
        for fetch in fetches:
            fetch.wait()
        wide_loads = raw_ref[...].astype(F32)
        loads_ref[...] = wide_loads
        basis_now = basis_ref[...]
        rows_now = rows_ref[...]
        packs = []
        for f, part in enumerate(split_faces(wide_loads)):
            packs.append(
                jnp.concatenate(
                    [part, basis_now[:, face * f : face * (f + 1)]]
                    + [rows_now[:, cols * c : cols * (c + 1)] for c in range(chunks)],
                    axis=0,
                )
            )
        give(outs, packs)

    outs = call(
        send_loads,
        [(field, F32), (basis.shape, F32), (coarse_rows.shape, F32)] + [((head, cols), F32)] * nrounds,
        [(field, BF16)],
        far=3,
        copies=3,
    )(loads, basis, coarse_rows)
    loads, basis, coarse_rows = outs[:3]
    got_a = trade(fill(outs[3:]))

    def reorder(first_hbm, second_hbm, map_ref, first_out, second_out, first_raw, second_raw, sems):
        fetches = [
            pltpu.make_async_copy(src, dst, sems.at[k])
            for k, (src, dst) in enumerate(((first_hbm, first_raw), (second_hbm, second_raw)))
        ]
        for fetch in fetches:
            fetch.start()
        slots = lax.broadcasted_iota(jnp.int32, (unknowns, unknowns), 0)
        pick = (slots == map_ref[...]).astype(F32).astype(BF16)
        for fetch, ref, out in zip(fetches, (first_raw, second_raw), (first_out, second_out)):
            fetch.wait()
            rows = half_dot(pick, ref[...]).astype(BF16)
            out[...] = lax.dot_general(
                rows, pick, (((1,), (1,)), ((), ())), preferred_element_type=F32
            ).astype(BF16)

    square = (unknowns, unknowns)
    inverse_here, schur_here = call(
        reorder,
        [(square, BF16)] * 2,
        [(square, BF16)] * 2,
        flops=8 * unknowns**3,
        moved=8 * unknowns**2,
        far=2,
        copies=2,
    )(local_inverse, schur, slot_map.reshape(1, unknowns))

    def first_local(*refs):
        got = take(spread(refs[:nrounds]))
        loads_ref, inverse_ref = refs[nrounds : nrounds + 2]
        res_ref, scaled_ref, product_ref, part_ref = refs[nrounds + 2 : nrounds + 6]
        sends = spread(refs[nrounds + 6 :])
        weights = face_weights()
        residual = add_faces(loads_ref[...], [g if g is None else g[:face] for g in got])
        scaled = weighted(residual, weights)
        product = half_dot(inverse_ref[...], scaled.astype(BF16))
        part = weighted(product, weights)
        give(sends, split_faces(part))
        res_ref[...] = residual
        scaled_ref[...] = scaled
        product_ref[...] = product
        part_ref[...] = part

    outs = call(first_local, [(field, F32)] * 4 + [face_out] * nrounds)(*got_a, loads, inverse_here)
    residual, scaled, product, part = outs[:4]
    got_b = trade(fill(outs[4:]))

    def first_coarse(basis_ref, scaled_ref, ci_ref):
        coarse_input = dot(basis_ref[...], scaled_ref[...])
        ci_ref[...] = jnp.broadcast_to(coarse_input[None], ci_ref.shape)

    (coarse_input,) = call(first_coarse, [((devices, nco, cols), F32)])(basis, scaled)
    coarse_all_in = lax.all_to_all(coarse_input, AXES, 0, 0).reshape(coarse_all, cols)

    def first_tables(*refs):
        got = take(spread(refs[:nrounds]))
        scaled_ref, product_ref, basis_ref, rows_ref = refs[nrounds : nrounds + 4]
        gram_ref, bases_ref, table_ref, wide_ref = refs[nrounds + 4 :]
        weights = face_weights()
        gram_ref[...] = dot(scaled_ref[...], product_ref[...], 0, 0)
        basis_now = basis_ref[...]
        bases, tables = [], []
        for f in range(4):
            mine = weights[f] * basis_now[:, face * f : face * (f + 1)]
            other = got[f]
            if other is None:
                bases += [mine, jnp.zeros_like(mine)]
                tables += [rows_ref[...], jnp.zeros((nco, coarse_all), F32)]
            else:
                bases += [mine, 0.5 * other[face : face + nco]]
                tables += [
                    rows_ref[...],
                    jnp.concatenate(
                        [
                            other[face + nco * (c + 1) : face + nco * (c + 2)]
                            for c in range(chunks)
                        ],
                        axis=1,
                    ),
                ]
        bases_ref[...] = jnp.concatenate(bases, axis=0)
        table_ref[...] = jnp.concatenate(tables, axis=0)
        src = lax.broadcasted_iota(jnp.int32, (cols, wide), 0)
        dst = lax.broadcasted_iota(jnp.int32, (cols, wide), 1)
        widen = (dst == src // nco * 8 + lax.rem(src, nco)).astype(F32)
        for c in range(chunks):
            wide_ref[:, wide * c : wide * (c + 1)] = dot(table_ref[:, cols * c : cols * (c + 1)], widen)

    wide = cols // nco * 8
    gram_part, bases, table, table_wide = call(
        first_tables,
        [
            (gram_shape, F32),
            ((8 * nco, face), F32),
            ((8 * nco, coarse_all), F32),
            ((8 * nco, wide * chunks), F32),
        ],
    )(*got_a, scaled, product, basis, coarse_rows)

    def coarse_part(bases_now, values):
        return [
            dot(bases_now[2 * nco * f : 2 * nco * (f + 1)], values[2 * nco * f : 2 * nco * (f + 1)], 0, 0)
            for f in range(4)
        ]

    per = 8 * -(-2 * cols // (8 * devices))
    blocks_out = ((devices, per, cols), F32)

    def first_direction(*refs):
        got = take(spread(refs[:nrounds]))
        part_ref, all_ref, bases_ref, table_ref, schur_ref = refs[nrounds : nrounds + 5]
        dir_ref, image_ref, values_ref = refs[nrounds + 5 : nrounds + 8]
        sends = spread(refs[nrounds + 8 :])
        values = dot(table_ref[...], all_ref[...])
        values_ref[...] = values
        coarse = coarse_part(bases_ref[...], values)
        update = add_faces(part_ref[...], got) + jnp.concatenate(coarse, axis=0)
        dir_ref[...] = update
        image = half_dot(schur_ref[...], update.astype(BF16))
        image_ref[...] = image
        give(sends, split_faces(image))

    outs = call(
        first_direction,
        [(field, F32), (field, F32), ((8 * nco, cols), F32)] + [face_out] * nrounds,
    )(*got_b, part, coarse_all_in, bases, table, schur_here)
    direction, image, values = outs[:3]
    got_d = trade(fill(outs[3:]))

    def first_grams(dir_ref, image_ref, values_ref, mine_ref, gram_ref, blocks_ref):
        first = gram_ref[...] + dot(mine_ref[0], values_ref[0:nco], 0, 0)
        curvature = dot(dir_ref[...], image_ref[...], 0, 0)
        write_blocks(blocks_ref, jnp.concatenate([curvature, first], axis=0))

    (blocks,) = call(first_grams, [blocks_out])(direction, image, values, coarse_input, gram_part)
    blocks = lax.all_to_all(blocks, AXES, 0, 0)

    def first_sums(*refs):
        got = take(spread(refs[:nrounds]))
        image_ref, blocks_ref, basis_ref = refs[nrounds : nrounds + 3]
        full_ref, sum_ref, mine_ref = refs[nrounds + 3 :]
        image_vec = add_faces(image_ref[...], got)
        full_ref[...] = image_vec
        coarse_image = dot(basis_ref[...], weighted(image_vec, face_weights()))
        mine_ref[...] = coarse_image
        block = jnp.concatenate(
            [jnp.sum(blocks_ref[...], axis=0), coarse_image, jnp.zeros((8 - nco, cols), F32)], axis=0
        )
        sum_ref[...] = jnp.broadcast_to(block[None], sum_ref.shape)

    image_vec, sums, coarse_image = call(
        first_sums,
        [(field, F32), ((devices, per + 8, cols), F32), ((nco, cols), F32)],
    )(*got_d, image, blocks, basis)
    sums = lax.all_to_all(sums, AXES, 0, 0)

    def second_local(sums_ref, res_ref, full_ref, inverse_ref, *outs):
        outs, work_ref = outs[:-1], outs[-1]
        curv_ref, first_ref, step_ref, scaled_ref, product_ref, part_ref = outs[:6]
        sends = spread(outs[6:])
        both = sums_ref[:, 0:per, :].reshape(devices * per, cols)
        curvature, first = both[:cols], both[cols : 2 * cols]
        step = solve(curvature, first, work_ref, (), 5)
        weights = face_weights()
        residual = res_ref[...] - dot(full_ref[...], step)
        scaled = weighted(residual, weights)
        product = half_dot(inverse_ref[...], scaled.astype(BF16))
        part = weighted(product, weights)
        part_ref[...] = part
        give(sends, split_faces(part))
        scaled_ref[...] = scaled
        product_ref[...] = product
        curv_ref[...] = curvature
        first_ref[...] = first
        step_ref[...] = step

    outs = call(
        second_local,
        [(gram_shape, F32)] * 3 + [(field, F32)] * 3 + [face_out] * nrounds,
        work,
    )(sums, residual, image_vec, inverse_here)
    curvature, first, step, scaled, product, part = outs[:6]
    got_e = trade(fill(outs[6:]))

    def second_coarse(
        sums_ref, table_ref, values_ref, mine_ref, image_ref, step_ref, scaled_ref, product_ref,
        next_ref, values_out
    ):
        rows = sums_ref[:, per : per + 8, :].reshape(devices * 8, cols)
        step = step_ref[...]
        values_now = values_ref[...] - dot(dot(table_ref[...], rows), step)
        values_out[...] = values_now
        own = mine_ref[0] - dot(image_ref[...], step)
        next_ref[...] = dot(scaled_ref[...], product_ref[...], 0, 0) + dot(own, values_now[:nco], 0, 0)

    next_part, values = call(
        second_coarse, [(gram_shape, F32), ((8 * nco, cols), F32)], flops=2 * 12 * unknowns * cols**2
    )(sums, table_wide, values, coarse_input, coarse_image, step, scaled, product)

    def second_direction(*refs):
        got = take(spread(refs[:nrounds]))
        part_ref, next_ref, values_ref, bases_ref, schur_ref = refs[nrounds : nrounds + 5]
        update_ref, blocks_ref = refs[nrounds + 5 :]
        coarse = coarse_part(bases_ref[...], values_ref[...])
        update = add_faces(part_ref[...], got) + jnp.concatenate(coarse, axis=0)
        update_ref[...] = update
        high = update.astype(BF16)
        low = (update - high.astype(F32)).astype(BF16)
        both = half_dot(schur_ref[...], jnp.concatenate([high, low], axis=1))
        product = both[:, :cols] + both[:, cols:]
        square = dot(update, product, 0, 0)
        write_blocks(blocks_ref, jnp.concatenate([next_ref[...], square], axis=0))

    update, blocks = call(second_direction, [(field, F32), blocks_out])(
        *got_e, part, next_part, values, bases, schur_here
    )
    blocks = lax.all_to_all(blocks, AXES, 0, 0)

    def invert(first_ref, out_ref, work_ref):
        size = first_ref.shape[0]
        row_id = lax.broadcasted_iota(jnp.int32, (size, size), 0)
        col_id = lax.broadcasted_iota(jnp.int32, (size, size), 1)
        out_ref[...] = solve(first_ref[...], (row_id == col_id).astype(F32), work_ref, (), 5)

    (first_inverse,) = call(invert, [(gram_shape, F32)], work, flops=2 * 60 * cols**3)(first)

    def second_sums(blocks_ref, out_ref):
        out_ref[...] = jnp.broadcast_to(jnp.sum(blocks_ref[...], axis=0)[None], out_ref.shape)

    (sums,) = call(second_sums, [blocks_out])(blocks)
    sums = lax.all_to_all(sums, AXES, 0, 0).reshape(devices * per, cols)

    def finish(sums_ref, first_ref, curv_ref, step_ref, dir_ref, update_ref, out_ref, work_ref):
        next_gram, square = sums_ref[0:cols], sums_ref[cols : 2 * cols]
        ratio = dot(first_ref[...], next_gram)
        curvature = square - dot(ratio, dot(curv_ref[...], ratio), 0, 0)
        step = solve(curvature, next_gram, work_ref, (1.8, 1.8, 1.5), 7)
        total = step_ref[...] + dot(ratio, step)
        out_ref[...] = dot(dir_ref[...], total) + dot(update_ref[...], step)

    (solved,) = call(finish, [(field, F32)], work)(
        sums, first_inverse, curvature, step, direction, update
    )
    return solved[None, None]


def solution(mesh):
    return jax.shard_map(
        local,
        mesh=mesh,
        in_specs=(
            P("gx", "gy", None, None),
            P("gx", "gy", None, None),
            P("gx", "gy", None, None),
            P("gx", "gy", None, None),
            P("gx", "gy", None, None),
            P("gx", "gy", None),
        ),
        out_specs=P("gx", "gy", None, None),
        check_vma=False,
    )
```

```python
import jax
import jax.numpy as jnp
from jax import lax
from jax.experimental import pallas as pl
from jax.experimental.pallas import tpu as pltpu
from jax.sharding import PartitionSpec as P

AXES = ("gx", "gy")
F32 = jnp.float32
BF16 = jnp.bfloat16
EXACT = lax.Precision.HIGHEST


def dot(left, right, left_dim=1, right_dim=0, precision=EXACT):
    return lax.dot_general(
        left,
        right,
        (((left_dim,), (right_dim,)), ((), ())),
        precision=precision,
        preferred_element_type=F32,
    )


def thirds(value):
    high = value.astype(BF16)
    rest = value - high.astype(F32)
    middle = rest.astype(BF16)
    return high, middle, (rest - middle.astype(F32)).astype(BF16)


def plain(left, right, left_dim=1, right_dim=0):
    return lax.dot_general(
        left, right, (((left_dim,), (right_dim,)), ((), ())), preferred_element_type=F32
    )


def deep_dot(left, right):
    a, b, c = thirds(left)
    p, q, r = thirds(right)
    return plain(
        jnp.concatenate([a, a, b, a, c, b], axis=1), jnp.concatenate([p, q, p, r, p, q], axis=0)
    )


def gram_dot(left, right):
    a, b, c = thirds(left)
    p, q, r = thirds(right)
    cols = right.shape[1]
    pair = jnp.concatenate([p, q], axis=1)
    first, second = plain(a, pair, 0, 0), plain(b, pair, 0, 0)
    small = second[:, cols:] + plain(a, r, 0, 0) + plain(c, p, 0, 0)
    return first[:, :cols] + (first[:, cols:] + second[:, :cols] + small)


def half_dot(left, right):
    return lax.dot_general(
        left, right, (((1,), (0,)), ((), ())), preferred_element_type=F32
    )


def call(body, outs, scratch=(), flops=0, moved=0, far=0, copies=0):
    sems = [pltpu.SemaphoreType.DMA((copies,))] if copies else []

    def run(*args):
        specs = [pl.BlockSpec(memory_space=pltpu.HBM if i < far else pltpu.VMEM) for i in range(len(args))]
        args = [pltpu.with_memory_space_constraint(a, pltpu.HBM) if i < far else a for i, a in enumerate(args)]
        return kernel_call(body, outs, scratch, flops, moved, sems, specs)(*args)

    return run


def kernel_call(body, outs, scratch, flops, moved, sems, specs):
    return pl.pallas_call(
        body,
        in_specs=specs,
        scratch_shapes=[pltpu.VMEM(shape, kind) for shape, kind in scratch] + sems,
        out_shape=[jax.ShapeDtypeStruct(shape, kind) for shape, kind in outs],
        compiler_params=pltpu.CompilerParams(vmem_limit_bytes=48 * 1024 * 1024),
        cost_estimate=pl.CostEstimate(flops=flops, bytes_accessed=moved, transcendentals=0),
    )


def pair_rounds(size):
    first = [(i, i + 1) for i in range(0, size - 1, 2)]
    second = [(i, i + 1) for i in range(1, size - 1, 2)]
    return [pairs + [(j, i) for i, j in pairs] for pairs in (second, first)]


def exchange(sends):
    got = []
    for axis, pieces in zip(AXES, (sends[0:2], sends[2:4])):
        for pairs, piece in zip(pair_rounds(lax.axis_size(axis)), pieces):
            got.append(lax.ppermute(piece, axis, pairs) if pairs else None)
    return got


def rounds_used():
    return [bool(p) for axis in AXES for p in pair_rounds(lax.axis_size(axis))]


def even(axis):
    return lax.rem(lax.axis_index(axis), 2) == 0


def to_rounds(faces):
    ex, ey = even("gx"), even("gy")
    return [
        jnp.where(ex, faces[0], faces[1]),
        jnp.where(ex, faces[1], faces[0]),
        jnp.where(ey, faces[2], faces[3]),
        jnp.where(ey, faces[3], faces[2]),
    ]


def to_faces(parts):
    ex, ey = even("gx"), even("gy")
    b, a, d, c = parts

    def choose(flag, yes, no):
        if yes is None and no is None:
            return None
        if yes is None:
            return jnp.where(flag, jnp.zeros_like(no), no)
        if no is None:
            return jnp.where(flag, yes, jnp.zeros_like(yes))
        return jnp.where(flag, yes, no)

    return [choose(ex, b, a), choose(ex, a, b), choose(ey, d, c), choose(ey, c, d)]


def face_weights():
    ix, iy = lax.axis_index("gx"), lax.axis_index("gy")
    shared = [
        ix > 0,
        ix < lax.axis_size("gx") - 1,
        iy > 0,
        iy < lax.axis_size("gy") - 1,
    ]
    return [jnp.where(flag, 0.5, 1.0).astype(F32) for flag in shared]


def split_faces(field):
    rows = field.shape[0] // 4
    return [field[rows * f : rows * (f + 1)] for f in range(4)]


def add_faces(field, got):
    faces = [
        mine if other is None else mine + other for mine, other in zip(split_faces(field), got)
    ]
    return jnp.concatenate(faces, axis=0)


def weighted(field, weights):
    return jnp.concatenate([w * v for w, v in zip(weights, split_faces(field))], axis=0)


def write_blocks(out_ref, rows):
    per = out_ref.shape[1]
    used = rows.shape[0] // per
    if used < out_ref.shape[0]:
        out_ref[...] = jnp.zeros(out_ref.shape, F32)
    out_ref[0:used] = rows.reshape(used, per, rows.shape[1])


def solve(matrix, right, work_ref, boosts, squarings):
    size = matrix.shape[0]
    row_id = lax.broadcasted_iota(jnp.int32, (size, size), 0)
    col_id = lax.broadcasted_iota(jnp.int32, (size, size), 1)
    eye = (row_id == col_id).astype(F32)
    only = matrix * eye
    by_row = lax.rsqrt(jnp.sum(only, axis=1, keepdims=True))
    by_col = lax.rsqrt(jnp.sum(only, axis=0, keepdims=True))
    unit = matrix * by_row * by_col
    bound = jnp.max(jnp.sum(jnp.abs(unit), axis=0, keepdims=True), axis=1, keepdims=True)
    scale = 1.9 / bound
    answer = right * (by_row * scale)
    power = eye - scale * unit

    def step(answer, power):
        return answer + deep_dot(power, answer), deep_dot(power, power)

    for k in range(squarings):
        answer, power = step(answer, power)
        if k < len(boosts):
            power = boosts[k] * power + (1.0 - boosts[k]) * eye
            answer = boosts[k] * answer
    work_ref[:, 0:size] = answer + deep_dot(power, answer)
    largest = jnp.max(jnp.abs(power))

    @pl.when(jnp.logical_not(largest < 3e-4))
    def _():
        work_ref[:, 0:size] = answer
        work_ref[:, size:] = power

        def again(carry):
            answer, power = step(work_ref[:, 0:size], work_ref[:, size:])
            work_ref[:, 0:size] = answer
            work_ref[:, size:] = power
            return carry[0] + 1, jnp.max(jnp.abs(power))

        lax.while_loop(
            lambda carry: jnp.logical_and(carry[0] < 40, carry[1] > 1e-7),
            again,
            (jnp.int32(0), largest),
        )

    return work_ref[:, 0:size] * by_row


def local(loads, schur, local_inverse, coarse_basis, coarse_inverse, face_map):
    loads, schur, local_inverse = loads[0, 0], schur[0, 0], local_inverse[0, 0]
    basis, coarse_rows, slot_map = coarse_basis[0, 0], coarse_inverse[0, 0], face_map[0, 0]
    unknowns, cols = loads.shape
    face = unknowns // 4
    nco, coarse_all = coarse_rows.shape
    devices = lax.axis_size("gx") * lax.axis_size("gy")
    chunks = coarse_all // cols
    used = rounds_used()
    field = (unknowns, cols)
    gram_shape = (cols, cols)
    work = [((cols, 2 * cols), F32)]
    face_out = ((face, cols), F32)

    def give(refs, faces):
        for ref, value, flag in zip(refs, to_rounds(faces), used):
            if flag:
                ref[...] = value

    def take(refs):
        return to_faces([ref[...] if flag else None for ref, flag in zip(refs, used)])

    def trade(sends):
        return [got for got in exchange(sends) if got is not None]

    def spread(refs):
        left = list(refs)
        return [left.pop(0) if flag else None for flag in used]

    nrounds = sum(used)

    def fill(values):
        left = list(values)
        return [left.pop(0) if flag else None for flag in used]

    head = face + nco + nco * chunks

    def send_loads(loads_hbm, basis_hbm, rows_hbm, map_hbm, loads_ref, basis_ref, rows_ref, map_ref, *outs):
        outs, raw_ref, sems = spread(outs[:-2]), outs[-2], outs[-1]
        fetches = [
            pltpu.make_async_copy(src, dst, sems.at[k])
            for k, (src, dst) in enumerate(
                ((loads_hbm, raw_ref), (basis_hbm, basis_ref), (rows_hbm, rows_ref), (map_hbm, map_ref))
            )
        ]
        for fetch in fetches:
            fetch.start()
        for fetch in fetches:
            fetch.wait()
        wide_loads = raw_ref[...].astype(F32)
        loads_ref[...] = wide_loads
        basis_now = basis_ref[...]
        rows_now = rows_ref[...]
        packs = []
        for f, part in enumerate(split_faces(wide_loads)):
            packs.append(
                jnp.concatenate(
                    [part, basis_now[:, face * f : face * (f + 1)]]
                    + [rows_now[:, cols * c : cols * (c + 1)] for c in range(chunks)],
                    axis=0,
                )
            )
        give(outs, packs)

    outs = call(
        send_loads,
        [(field, F32), (basis.shape, F32), (coarse_rows.shape, F32), ((1, unknowns), jnp.int32)]
        + [((head, cols), F32)] * nrounds,
        [(field, BF16)],
        far=4,
        copies=4,
    )(loads, basis, coarse_rows, slot_map.reshape(1, unknowns))
    loads, basis, coarse_rows, slot_map = outs[:4]
    got_a = trade(fill(outs[4:]))

    def reorder(first_hbm, second_hbm, map_ref, first_out, second_out, first_raw, second_raw, sems):
        fetches = [
            pltpu.make_async_copy(src, dst, sems.at[k])
            for k, (src, dst) in enumerate(((first_hbm, first_raw), (second_hbm, second_raw)))
        ]
        for fetch in fetches:
            fetch.start()
        slots = lax.broadcasted_iota(jnp.int32, (unknowns, unknowns), 0)
        pick = (slots == map_ref[...]).astype(F32).astype(BF16)
        for fetch, ref, out in zip(fetches, (first_raw, second_raw), (first_out, second_out)):
            fetch.wait()
            rows = half_dot(pick, ref[...]).astype(BF16)
            out[...] = lax.dot_general(
                rows, pick, (((1,), (1,)), ((), ())), preferred_element_type=F32
            ).astype(BF16)

    square = (unknowns, unknowns)
    inverse_here, schur_here = call(
        reorder,
        [(square, BF16)] * 2,
        [(square, BF16)] * 2,
        flops=8 * unknowns**3,
        moved=8 * unknowns**2,
        far=2,
        copies=2,
    )(local_inverse, schur, slot_map)

    def first_local(*refs):
        got = take(spread(refs[:nrounds]))
        loads_ref, inverse_ref, basis_ref = refs[nrounds : nrounds + 3]
        res_ref, scaled_ref, product_ref, part_ref, ci_ref = refs[nrounds + 3 : nrounds + 8]
        sends = spread(refs[nrounds + 8 :])
        weights = face_weights()
        residual = add_faces(loads_ref[...], [g if g is None else g[:face] for g in got])
        scaled = weighted(residual, weights)
        product = half_dot(inverse_ref[...], scaled.astype(BF16))
        part = weighted(product, weights)
        give(sends, split_faces(part))
        coarse_input = dot(basis_ref[...], scaled)
        ci_ref[...] = jnp.broadcast_to(coarse_input[None], ci_ref.shape)
        res_ref[...] = residual
        scaled_ref[...] = scaled
        product_ref[...] = product
        part_ref[...] = part

    outs = call(
        first_local, [(field, F32)] * 4 + [((devices, nco, cols), F32)] + [face_out] * nrounds
    )(*got_a, loads, inverse_here, basis)
    residual, scaled, product, part, coarse_input = outs[:5]
    got_b = trade(fill(outs[5:]))
    coarse_all_in = lax.all_to_all(coarse_input, AXES, 0, 0).reshape(coarse_all, cols)

    def first_tables(*refs):
        got = take(spread(refs[:nrounds]))
        scaled_ref, product_ref, basis_ref, rows_ref = refs[nrounds : nrounds + 4]
        gram_ref, bases_ref, table_ref = refs[nrounds + 4 :]
        weights = face_weights()
        gram_ref[...] = gram_dot(scaled_ref[...], product_ref[...])
        basis_now = basis_ref[...]
        bases, tables = [], []
        for f in range(4):
            mine = weights[f] * basis_now[:, face * f : face * (f + 1)]
            other = got[f]
            if other is None:
                bases += [mine, jnp.zeros_like(mine)]
                tables += [rows_ref[...], jnp.zeros((nco, coarse_all), F32)]
            else:
                bases += [mine, 0.5 * other[face : face + nco]]
                tables += [
                    rows_ref[...],
                    jnp.concatenate(
                        [
                            other[face + nco * (c + 1) : face + nco * (c + 2)]
                            for c in range(chunks)
                        ],
                        axis=1,
                    ),
                ]
        bases_ref[...] = jnp.concatenate(bases, axis=0)
        table_ref[...] = jnp.concatenate(tables, axis=0)

    gram_part, bases, table = call(
        first_tables,
        [
            (gram_shape, F32),
            ((8 * nco, face), F32),
            ((8 * nco, coarse_all), F32),
        ],
    )(*got_a, scaled, product, basis, coarse_rows)

    def coarse_part(bases_now, values):
        return [
            dot(bases_now[2 * nco * f : 2 * nco * (f + 1)], values[2 * nco * f : 2 * nco * (f + 1)], 0, 0)
            for f in range(4)
        ]

    mine = -(-cols // devices)
    packers = cols // mine
    packed = 8 * -(-(mine + 1) // 8)

    def triangles():
        row_id = lax.broadcasted_iota(jnp.int32, gram_shape, 0)
        col_id = lax.broadcasted_iota(jnp.int32, gram_shape, 1)
        return row_id < col_id, row_id == col_id

    def first_direction(*refs):
        got = take(spread(refs[:nrounds]))
        part_ref, all_ref, bases_ref, table_ref, schur_ref, mine_ref, gram_ref = refs[nrounds : nrounds + 7]
        dir_ref, image_ref, values_ref, blocks_ref = refs[nrounds + 7 : nrounds + 11]
        sends = spread(refs[nrounds + 11 :])
        values = dot(table_ref[...], all_ref[...])
        values_ref[...] = values
        coarse = coarse_part(bases_ref[...], values)
        update = add_faces(part_ref[...], got) + jnp.concatenate(coarse, axis=0)
        dir_ref[...] = update
        image = half_dot(schur_ref[...], update.astype(BF16))
        image_ref[...] = image
        give(sends, split_faces(image))
        first = gram_ref[...] + dot(mine_ref[0], values[:nco], 0, 0)
        curvature = gram_dot(update, image)
        above, on = triangles()
        both = jnp.where(above, curvature + curvature.T, first + first.T) * 0.5
        diagonal = jnp.sum(jnp.where(on, curvature, 0.0), axis=0, keepdims=True)
        blocks_ref[:, mine : mine + 1, :] = jnp.broadcast_to(diagonal[None], (devices, 1, cols))
        if packers < devices:
            blocks_ref[:, 0:mine, :] = jnp.zeros((devices, mine, cols), F32)
        if mine + 1 < packed:
            blocks_ref[:, mine + 1 :, :] = jnp.zeros((devices, packed - mine - 1, cols), F32)
        for k in range(packers):
            blocks_ref[k, 0:mine, :] = both[mine * k : mine * (k + 1)]

    outs = call(
        first_direction,
        [(field, F32), (field, F32), ((8 * nco, cols), F32), ((devices, packed, cols), F32)]
        + [face_out] * nrounds,
    )(*got_b, part, coarse_all_in, bases, table, schur_here, coarse_input, gram_part)
    direction, image, values, blocks = outs[:4]
    got_d = trade(fill(outs[4:]))
    blocks = lax.all_to_all(blocks, AXES, 0, 0)
    joint = 8 * -(-(mine + nco) // 8)

    def first_sums(*refs):
        got = take(spread(refs[:nrounds]))
        image_ref, blocks_ref, basis_ref = refs[nrounds : nrounds + 3]
        full_ref, sum_ref, mine_ref, diag_ref = refs[nrounds + 3 :]
        image_vec = add_faces(image_ref[...], got)
        full_ref[...] = image_vec
        coarse_image = dot(basis_ref[...], weighted(image_vec, face_weights()))
        mine_ref[...] = coarse_image
        total = jnp.sum(blocks_ref[...], axis=0)
        diag_ref[...] = total[mine : mine + 1]
        rows = [total[0:mine], coarse_image]
        if mine + nco < joint:
            rows.append(jnp.zeros((joint - mine - nco, cols), F32))
        sum_ref[...] = jnp.broadcast_to(jnp.concatenate(rows, axis=0)[None], sum_ref.shape)

    image_vec, sums, coarse_image, diagonal = call(
        first_sums,
        [(field, F32), ((devices, joint, cols), F32), ((nco, cols), F32), ((1, cols), F32)],
    )(*got_d, image, blocks, basis)
    sums = lax.all_to_all(sums, AXES, 0, 0)

    def second_local(sums_ref, diag_ref, res_ref, full_ref, inverse_ref, *outs):
        outs, work_ref = outs[:-1], outs[-1]
        curv_ref, first_ref, step_ref, scaled_ref, product_ref, part_ref = outs[:6]
        sends = spread(outs[6:])
        both = jnp.concatenate([sums_ref[k, 0:mine, :] for k in range(packers)], axis=0)
        turned = both.T
        above, on = triangles()
        curvature = jnp.where(above, both, jnp.where(on, diag_ref[...], turned))
        first = jnp.where(above, turned, both)
        step = solve(curvature, first, work_ref, (), 5)
        weights = face_weights()
        residual = res_ref[...] - dot(full_ref[...], step)
        scaled = weighted(residual, weights)
        product = half_dot(inverse_ref[...], scaled.astype(BF16))
        part = weighted(product, weights)
        part_ref[...] = part
        give(sends, split_faces(part))
        scaled_ref[...] = scaled
        product_ref[...] = product
        curv_ref[...] = curvature
        first_ref[...] = first
        step_ref[...] = step

    outs = call(
        second_local,
        [(gram_shape, F32)] * 3 + [(field, F32)] * 3 + [face_out] * nrounds,
        work,
    )(sums, diagonal, residual, image_vec, inverse_here)
    curvature, first, step, scaled, product, part = outs[:6]
    got_e = trade(fill(outs[6:]))

    def second_coarse(
        sums_ref, table_ref, values_ref, mine_ref, image_ref, step_ref, scaled_ref, product_ref,
        first_ref, curv_ref, next_ref, values_out, inv_ref, quad_ref, work_ref
    ):
        rows = jnp.concatenate([sums_ref[k, mine : mine + nco, :] for k in range(devices)], axis=0)
        step = step_ref[...]
        values_now = values_ref[...] - dot(dot(table_ref[...], rows), step)
        values_out[...] = values_now
        own = mine_ref[0] - dot(image_ref[...], step)
        next_ref[...] = gram_dot(scaled_ref[...], product_ref[...]) + dot(own, values_now[:nco], 0, 0)
        _, on = triangles()
        inverse = solve(first_ref[...], on.astype(F32), work_ref, (), 4)
        inv_ref[...] = inverse
        quad_ref[...] = gram_dot(inverse, deep_dot(curv_ref[...], inverse))

    next_part, values, first_inverse, quad = call(
        second_coarse,
        [(gram_shape, F32), ((8 * nco, cols), F32), (gram_shape, F32), (gram_shape, F32)],
        work,
        flops=2 * 12 * unknowns * cols**2,
    )(sums, table, values, coarse_input, coarse_image, step, scaled, product, first, curvature)

    per = 8 * -(-2 * cols // (8 * devices))
    blocks_out = ((devices, per, cols), F32)

    def second_direction(*refs):
        got = take(spread(refs[:nrounds]))
        part_ref, next_ref, values_ref, bases_ref, schur_ref = refs[nrounds : nrounds + 5]
        update_ref, blocks_ref = refs[nrounds + 5 :]
        coarse = coarse_part(bases_ref[...], values_ref[...])
        update = add_faces(part_ref[...], got) + jnp.concatenate(coarse, axis=0)
        update_ref[...] = update
        high = update.astype(BF16)
        low = (update - high.astype(F32)).astype(BF16)
        both = half_dot(schur_ref[...], jnp.concatenate([high, low], axis=1))
        product = both[:, :cols] + both[:, cols:]
        square = gram_dot(update, product)
        write_blocks(blocks_ref, jnp.concatenate([next_ref[...], square], axis=0))

    update, blocks = call(second_direction, [(field, F32), blocks_out])(
        *got_e, part, next_part, values, bases, schur_here
    )
    blocks = lax.all_to_all(blocks, AXES, 0, 0)

    def second_sums(blocks_ref, out_ref, keep_ref):
        total = jnp.sum(blocks_ref[...], axis=0)
        out_ref[...] = jnp.broadcast_to(total[None], out_ref.shape)
        keep_ref[...] = total

    sums, _ = call(second_sums, [blocks_out, ((per, cols), F32)])(blocks)
    sums = lax.all_to_all(sums, AXES, 0, 0).reshape(devices * per, cols)

    def finish(sums_ref, inv_ref, quad_ref, step_ref, dir_ref, update_ref, out_ref, work_ref):
        next_gram, square = sums_ref[0:cols], sums_ref[cols : 2 * cols]
        curvature = square - gram_dot(next_gram, deep_dot(quad_ref[...], next_gram))
        curvature = 0.5 * (curvature + curvature.T)
        ratio = deep_dot(inv_ref[...], next_gram)
        step = solve(curvature, next_gram, work_ref, (1.8, 1.8, 1.5), 7)
        total = step_ref[...] + deep_dot(ratio, step)
        fields = jnp.concatenate([dir_ref[...], update_ref[...]], axis=1)
        coefs = jnp.concatenate([total, step], axis=0)
        a, b, _ = thirds(fields)
        p, q, _ = thirds(coefs)
        out_ref[...] = plain(a, p) + (plain(a, q) + plain(b, p))

    (solved,) = call(finish, [(field, F32)], work)(
        sums, first_inverse, quad, step, direction, update
    )
    return solved[None, None]


def solution(mesh):
    return jax.shard_map(
        local,
        mesh=mesh,
        in_specs=(
            P("gx", "gy", None, None),
            P("gx", "gy", None, None),
            P("gx", "gy", None, None),
            P("gx", "gy", None, None),
            P("gx", "gy", None, None),
            P("gx", "gy", None),
        ),
        out_specs=P("gx", "gy", None, None),
        check_vma=False,
    )
```

```python
import jax
import jax.numpy as jnp
from jax import lax
from jax.experimental import pallas as pl
from jax.experimental.pallas import tpu as pltpu
from jax.sharding import PartitionSpec as P

AXES = ("gx", "gy")
F32 = jnp.float32
BF16 = jnp.bfloat16
EXACT = lax.Precision.HIGHEST


def dot(left, right, left_dim=1, right_dim=0, precision=EXACT):
    return lax.dot_general(
        left,
        right,
        (((left_dim,), (right_dim,)), ((), ())),
        precision=precision,
        preferred_element_type=F32,
    )


def thirds(value):
    high = value.astype(BF16)
    rest = value - high.astype(F32)
    middle = rest.astype(BF16)
    return high, middle, (rest - middle.astype(F32)).astype(BF16)


def plain(left, right, left_dim=1, right_dim=0):
    return lax.dot_general(
        left, right, (((left_dim,), (right_dim,)), ((), ())), preferred_element_type=F32
    )


def deep_dot(left, right):
    a, b, c = thirds(left)
    p, q, r = thirds(right)
    return plain(
        jnp.concatenate([a, a, b, a, c, b], axis=1), jnp.concatenate([p, q, p, r, p, q], axis=0)
    )


def gram_dot(left, right):
    a, b, _ = thirds(left)
    p, q, _ = thirds(right)
    cols = right.shape[1]
    pair = plain(a, jnp.concatenate([p, q], axis=1), 0, 0)
    return pair[:, :cols] + (pair[:, cols:] + plain(b, p, 0, 0))


def flat_dot(left, right):
    a, b, _ = thirds(left)
    p, q, _ = thirds(right)
    return plain(jnp.concatenate([a, a, b], axis=1), jnp.concatenate([p, q, p], axis=0))


def half_dot(left, right):
    return lax.dot_general(
        left, right, (((1,), (0,)), ((), ())), preferred_element_type=F32
    )


def call(body, outs, scratch=(), flops=0, moved=0, far=0, copies=0, far_out=False):
    sems = [pltpu.SemaphoreType.DMA((copies,))] if copies else []

    def run(*args):
        specs = [pl.BlockSpec(memory_space=pltpu.HBM if i < far else pltpu.VMEM) for i in range(len(args))]
        args = [pltpu.with_memory_space_constraint(a, pltpu.HBM) if i < far else a for i, a in enumerate(args)]
        results = [pl.BlockSpec(memory_space=pltpu.HBM if far_out else pltpu.VMEM) for _ in outs]
        return kernel_call(body, outs, scratch, flops, moved, sems, specs, results)(*args)

    return run


def kernel_call(body, outs, scratch, flops, moved, sems, specs, results):
    return pl.pallas_call(
        body,
        in_specs=specs,
        out_specs=results,
        scratch_shapes=[pltpu.VMEM(shape, kind) for shape, kind in scratch] + sems,
        out_shape=[jax.ShapeDtypeStruct(shape, kind) for shape, kind in outs],
        compiler_params=pltpu.CompilerParams(vmem_limit_bytes=48 * 1024 * 1024),
        cost_estimate=pl.CostEstimate(flops=flops, bytes_accessed=moved, transcendentals=0),
    )


def pair_rounds(size):
    first = [(i, i + 1) for i in range(0, size - 1, 2)]
    second = [(i, i + 1) for i in range(1, size - 1, 2)]
    return [pairs + [(j, i) for i, j in pairs] for pairs in (second, first)]


def exchange(sends):
    got = []
    for axis, pieces in zip(AXES, (sends[0:2], sends[2:4])):
        for pairs, piece in zip(pair_rounds(lax.axis_size(axis)), pieces):
            got.append(lax.ppermute(piece, axis, pairs) if pairs else None)
    return got


def rounds_used():
    return [bool(p) for axis in AXES for p in pair_rounds(lax.axis_size(axis))]


def even(axis):
    return lax.rem(lax.axis_index(axis), 2) == 0


def to_rounds(faces):
    ex, ey = even("gx"), even("gy")
    return [
        jnp.where(ex, faces[0], faces[1]),
        jnp.where(ex, faces[1], faces[0]),
        jnp.where(ey, faces[2], faces[3]),
        jnp.where(ey, faces[3], faces[2]),
    ]


def to_faces(parts):
    ex, ey = even("gx"), even("gy")
    b, a, d, c = parts

    def choose(flag, yes, no):
        if yes is None and no is None:
            return None
        if yes is None:
            return jnp.where(flag, jnp.zeros_like(no), no)
        if no is None:
            return jnp.where(flag, yes, jnp.zeros_like(yes))
        return jnp.where(flag, yes, no)

    return [choose(ex, b, a), choose(ex, a, b), choose(ey, d, c), choose(ey, c, d)]


def face_weights():
    ix, iy = lax.axis_index("gx"), lax.axis_index("gy")
    shared = [
        ix > 0,
        ix < lax.axis_size("gx") - 1,
        iy > 0,
        iy < lax.axis_size("gy") - 1,
    ]
    return [jnp.where(flag, 0.5, 1.0).astype(F32) for flag in shared]


def split_faces(field):
    rows = field.shape[0] // 4
    return [field[rows * f : rows * (f + 1)] for f in range(4)]


def add_faces(field, got):
    faces = [
        mine if other is None else mine + other for mine, other in zip(split_faces(field), got)
    ]
    return jnp.concatenate(faces, axis=0)


def weighted(field, weights):
    return jnp.concatenate([w * v for w, v in zip(weights, split_faces(field))], axis=0)


def write_blocks(out_ref, rows):
    per = out_ref.shape[1]
    used = rows.shape[0] // per
    if used < out_ref.shape[0]:
        out_ref[...] = jnp.zeros(out_ref.shape, F32)
    out_ref[0:used] = rows.reshape(used, per, rows.shape[1])


def solve(matrix, right, work_ref, boosts, squarings):
    size = matrix.shape[0]
    row_id = lax.broadcasted_iota(jnp.int32, (size, size), 0)
    col_id = lax.broadcasted_iota(jnp.int32, (size, size), 1)
    eye = (row_id == col_id).astype(F32)
    only = matrix * eye
    by_row = lax.rsqrt(jnp.sum(only, axis=1, keepdims=True))
    by_col = lax.rsqrt(jnp.sum(only, axis=0, keepdims=True))
    unit = matrix * by_row * by_col
    bound = jnp.max(jnp.sum(jnp.abs(unit), axis=0, keepdims=True), axis=1, keepdims=True)
    scale = 1.9 / bound
    answer = right * (by_row * scale)
    power = eye - scale * unit

    def step(answer, power, product=deep_dot):
        return answer + product(power, answer), product(power, power)

    for k in range(squarings):
        answer, power = step(answer, power, flat_dot if boosts and k > 1 else deep_dot)
        if k < len(boosts):
            power = boosts[k] * power + (1.0 - boosts[k]) * eye
            answer = boosts[k] * answer
    work_ref[:, 0:size] = answer + deep_dot(power, answer)
    largest = jnp.max(jnp.abs(power))

    @pl.when(jnp.logical_not(largest < 3e-4))
    def _():
        work_ref[:, 0:size] = answer
        work_ref[:, size:] = power

        def again(carry):
            answer, power = step(work_ref[:, 0:size], work_ref[:, size:])
            work_ref[:, 0:size] = answer
            work_ref[:, size:] = power
            return carry[0] + 1, jnp.max(jnp.abs(power))

        lax.while_loop(
            lambda carry: jnp.logical_and(carry[0] < 40, carry[1] > 1e-7),
            again,
            (jnp.int32(0), largest),
        )

    return work_ref[:, 0:size] * by_row


def local(loads, schur, local_inverse, coarse_basis, coarse_inverse, face_map):
    loads, schur, local_inverse = loads[0, 0], schur[0, 0], local_inverse[0, 0]
    basis, coarse_rows, slot_map = coarse_basis[0, 0], coarse_inverse[0, 0], face_map[0, 0]
    unknowns, cols = loads.shape
    face = unknowns // 4
    nco, coarse_all = coarse_rows.shape
    devices = lax.axis_size("gx") * lax.axis_size("gy")
    chunks = coarse_all // cols
    used = rounds_used()
    field = (unknowns, cols)
    gram_shape = (cols, cols)
    work = [((cols, 2 * cols), F32)]
    face_out = ((face, cols), F32)

    def give(refs, faces):
        for ref, value, flag in zip(refs, to_rounds(faces), used):
            if flag:
                ref[...] = value

    def take(refs):
        return to_faces([ref[...] if flag else None for ref, flag in zip(refs, used)])

    def trade(sends):
        return [got for got in exchange(sends) if got is not None]

    def spread(refs):
        left = list(refs)
        return [left.pop(0) if flag else None for flag in used]

    nrounds = sum(used)

    def fill(values):
        left = list(values)
        return [left.pop(0) if flag else None for flag in used]

    head = face + nco + nco * chunks

    def send_loads(loads_hbm, basis_hbm, rows_hbm, map_hbm, loads_ref, basis_ref, rows_ref, map_ref, *outs):
        outs, raw_ref, sems = spread(outs[:-2]), outs[-2], outs[-1]
        fetches = [
            pltpu.make_async_copy(src, dst, sems.at[k])
            for k, (src, dst) in enumerate(
                ((loads_hbm, raw_ref), (basis_hbm, basis_ref), (rows_hbm, rows_ref), (map_hbm, map_ref))
            )
        ]
        for fetch in fetches:
            fetch.start()
        for fetch in fetches:
            fetch.wait()
        wide_loads = raw_ref[...].astype(F32)
        loads_ref[...] = wide_loads
        basis_now = basis_ref[...]
        rows_now = rows_ref[...]
        packs = []
        for f, part in enumerate(split_faces(wide_loads)):
            packs.append(
                jnp.concatenate(
                    [part, basis_now[:, face * f : face * (f + 1)]]
                    + [rows_now[:, cols * c : cols * (c + 1)] for c in range(chunks)],
                    axis=0,
                )
            )
        give(outs, packs)

    outs = call(
        send_loads,
        [(field, F32), (basis.shape, F32), (coarse_rows.shape, F32), ((1, unknowns), jnp.int32)]
        + [((head, cols), F32)] * nrounds,
        [(field, BF16)],
        far=4,
        copies=4,
    )(loads, basis, coarse_rows, slot_map.reshape(1, unknowns))
    loads, basis, coarse_rows, slot_map = outs[:4]
    got_a = trade(fill(outs[4:]))

    square = (unknowns, unknowns)

    def reorder(first_hbm, second_hbm, map_ref, first_out, second_out, first_raw, second_raw, sems):
        fetches = [
            pltpu.make_async_copy(src, dst, sems.at[k])
            for k, (src, dst) in enumerate(((first_hbm, first_raw), (second_hbm, second_raw)))
        ]
        for fetch in fetches:
            fetch.start()
        slots = lax.broadcasted_iota(jnp.int32, square, 0)
        pick = (slots == map_ref[...]).astype(F32).astype(BF16)
        for fetch, ref, out in zip(fetches, (first_raw, second_raw), (first_out, second_out)):
            fetch.wait()
            rows = half_dot(pick, ref[...]).astype(BF16)
            out[...] = plain(rows, pick, 1, 1).astype(BF16)

    inverse_here, schur_here = call(
        reorder,
        [(square, BF16)] * 2,
        [(square, BF16)] * 2,
        flops=8 * unknowns**3,
        moved=8 * unknowns**2,
        far=2,
        copies=2,
    )(local_inverse, schur, slot_map)

    def first_local(*refs):
        got = take(spread(refs[:nrounds]))
        loads_ref, inverse_ref, basis_ref = refs[nrounds : nrounds + 3]
        res_ref, scaled_ref, product_ref, part_ref, ci_ref = refs[nrounds + 3 : nrounds + 8]
        sends = spread(refs[nrounds + 8 :])
        weights = face_weights()
        residual = add_faces(loads_ref[...], [g if g is None else g[:face] for g in got])
        scaled = weighted(residual, weights)
        product = half_dot(inverse_ref[...], scaled.astype(BF16))
        part = weighted(product, weights)
        give(sends, split_faces(part))
        coarse_input = dot(basis_ref[...], scaled)
        ci_ref[...] = jnp.broadcast_to(coarse_input[None], ci_ref.shape)
        res_ref[...] = residual
        scaled_ref[...] = scaled
        product_ref[...] = product
        part_ref[...] = part

    outs = call(
        first_local, [(field, F32)] * 4 + [((devices, nco, cols), F32)] + [face_out] * nrounds
    )(*got_a, loads, inverse_here, basis)
    residual, scaled, product, part, coarse_input = outs[:5]
    got_b = trade(fill(outs[5:]))
    coarse_all_in = lax.all_to_all(coarse_input, AXES, 0, 0).reshape(coarse_all, cols)

    def first_tables(*refs):
        got = take(spread(refs[:nrounds]))
        scaled_ref, product_ref, basis_ref, rows_ref = refs[nrounds : nrounds + 4]
        gram_ref, bases_ref, deep_ref, table_ref = refs[nrounds + 4 :]
        weights = face_weights()
        gram_ref[...] = gram_dot(scaled_ref[...], product_ref[...])
        basis_now = basis_ref[...]
        bases, tables = [], []
        for f in range(4):
            mine_now = weights[f] * basis_now[:, face * f : face * (f + 1)]
            other = got[f]
            if other is None:
                both = [mine_now, jnp.zeros_like(mine_now)]
                tables += [rows_ref[...], jnp.zeros((nco, coarse_all), F32)]
            else:
                both = [mine_now, 0.5 * other[face : face + nco]]
                tables += [
                    rows_ref[...],
                    jnp.concatenate(
                        [
                            other[face + nco * (c + 1) : face + nco * (c + 2)]
                            for c in range(chunks)
                        ],
                        axis=1,
                    ),
                ]
            none = jnp.zeros((2 * nco, face), F32)
            block = jnp.concatenate(both, axis=0)
            bases.append(jnp.concatenate([block if k == f else none for k in range(4)], axis=1))
        by_row = jnp.concatenate(bases, axis=0).T
        bases_ref[...] = by_row
        a, b, c = thirds(by_row)
        deep_ref[...] = jnp.concatenate([a, a, b, a, c, b], axis=1)
        table_ref[...] = jnp.concatenate(tables, axis=0)

    gram_part, bases, deep_bases, table = call(
        first_tables,
        [
            (gram_shape, F32),
            ((unknowns, 8 * nco), F32),
            ((unknowns, 48 * nco), BF16),
            ((8 * nco, coarse_all), F32),
        ],
    )(*got_a, scaled, product, basis, coarse_rows)

    def coarse_part(deep, values):
        p, q, r = thirds(values)
        return plain(deep, jnp.concatenate([p, q, p, r, p, q], axis=0))

    mine = -(-cols // devices)
    packers = cols // mine
    packed = mine + 1 + nco

    def triangles():
        row_id = lax.broadcasted_iota(jnp.int32, gram_shape, 0)
        col_id = lax.broadcasted_iota(jnp.int32, gram_shape, 1)
        return row_id < col_id, row_id == col_id

    def first_coarse(all_ref, deep_ref, table_ref, mine_ref, gram_ref, values_ref, coarse_ref, first_ref):
        values = deep_dot(table_ref[...], all_ref[...])
        values_ref[...] = values
        coarse_ref[...] = coarse_part(deep_ref[...], values)
        first = gram_ref[...] + dot(mine_ref[0], values[:nco], 0, 0)
        first_ref[...] = 0.5 * (first + first.T)

    values, coarse, first_part = call(
        first_coarse, [((8 * nco, cols), F32), (field, F32), (gram_shape, F32)]
    )(coarse_all_in, deep_bases, table, coarse_input, gram_part)

    def first_direction(*refs):
        got = take(spread(refs[:nrounds]))
        part_ref, coarse_ref, bases_ref, schur_ref, first_ref = refs[nrounds : nrounds + 5]
        dir_ref, image_ref, blocks_ref = refs[nrounds + 5 : nrounds + 8]
        sends = spread(refs[nrounds + 8 :])
        if packers < devices:
            blocks_ref[...] = jnp.zeros(blocks_ref.shape, F32)
        else:
            blocks_ref[:, mine + 1 :] = jnp.zeros((devices, nco, 1, cols), F32)
        update = add_faces(part_ref[...], got) + coarse_ref[...]
        dir_ref[...] = update
        image = half_dot(schur_ref[...], update.astype(BF16))
        image_ref[...] = image
        give(sends, split_faces(image))
        stack = gram_dot(jnp.concatenate([update, bases_ref[...]], axis=1), image)
        curvature, shares = stack[:cols], stack[cols:]
        above, on = triangles()
        both = jnp.where(above, 0.5 * (curvature + curvature.T), first_ref[...])
        diagonal = jnp.sum(jnp.where(on, curvature, 0.0), axis=0, keepdims=True)
        blocks_ref[:, mine : mine + 1] = jnp.broadcast_to(
            diagonal.reshape(1, 1, 1, cols), (devices, 1, 1, cols)
        )
        for k in range(packers):
            for r in range(mine):
                blocks_ref[k, r] = both[mine * k + r : mine * k + r + 1]
        ix, iy = lax.axis_index("gx"), lax.axis_index("gy")
        sx, sy = lax.axis_size("gx"), lax.axis_size("gy")
        own = shares[0:nco]
        for f in range(1, 4):
            own = own + shares[2 * nco * f : 2 * nco * f + nco]
        here = ix * sy + iy
        targets = [
            (here, own, None),
            (here - sy, shares[nco : 2 * nco], ix > 0),
            (here + sy, shares[3 * nco : 4 * nco], ix < sx - 1),
            (here - 1, shares[5 * nco : 6 * nco], iy > 0),
            (here + 1, shares[7 * nco : 8 * nco], iy < sy - 1),
        ]

        def put(target, rows):
            for r in range(nco):
                blocks_ref[target, mine + 1 + r] = rows[r : r + 1]

        for target, rows, flag in targets:
            if flag is None:
                put(target, rows)
            else:
                pl.when(flag)(lambda target=target, rows=rows: put(target, rows))

    outs = call(
        first_direction,
        [(field, F32), (field, F32), ((devices, packed, 1, cols), F32)] + [face_out] * nrounds,
    )(*got_b, part, coarse, bases, schur_here, first_part)
    direction, image, blocks = outs[:3]
    got_d = trade(fill(outs[3:]))
    blocks = lax.all_to_all(blocks, AXES, 0, 0)
    joint = 8 * -(-(mine + nco) // 8)

    def first_sums(blocks_ref, sum_ref, mine_ref, diag_ref):
        total = jnp.sum(blocks_ref[...], axis=0)
        diag_ref[...] = total[mine]
        coarse_image = [total[mine + 1 + r] for r in range(nco)]
        mine_ref[...] = jnp.concatenate(coarse_image, axis=0)
        rows = [total[r] for r in range(mine)] + coarse_image
        if mine + nco < joint:
            rows.append(jnp.zeros((joint - mine - nco, cols), F32))
        sum_ref[...] = jnp.broadcast_to(jnp.concatenate(rows, axis=0)[None], sum_ref.shape)

    sums, coarse_image, diagonal = call(
        first_sums,
        [((devices, joint, cols), F32), ((nco, cols), F32), ((1, cols), F32)],
    )(blocks)
    sums = lax.all_to_all(sums, AXES, 0, 0)

    def first_step(sums_ref, diag_ref, curv_ref, first_ref, step_ref, work_ref):
        both = jnp.concatenate([sums_ref[k, 0:mine, :] for k in range(packers)], axis=0)
        turned = both.T
        above, on = triangles()
        curvature = jnp.where(above, both, jnp.where(on, diag_ref[...], turned))
        first = jnp.where(above, turned, both)
        step_ref[...] = solve(curvature, first, work_ref, (), 5)
        curv_ref[...] = curvature
        first_ref[...] = first

    curvature, first, step = call(first_step, [(gram_shape, F32)] * 3, work, flops=2 * 12 * cols**3)(
        sums, diagonal
    )

    def second_local(*refs):
        got = take(spread(refs[:nrounds]))
        step_ref, res_ref, image_ref, inverse_ref = refs[nrounds : nrounds + 4]
        scaled_ref, product_ref, part_ref = refs[nrounds + 4 : nrounds + 7]
        sends = spread(refs[nrounds + 7 :])
        weights = face_weights()
        residual = res_ref[...] - dot(add_faces(image_ref[...], got), step_ref[...])
        scaled = weighted(residual, weights)
        product = half_dot(inverse_ref[...], scaled.astype(BF16))
        part = weighted(product, weights)
        part_ref[...] = part
        give(sends, split_faces(part))
        scaled_ref[...] = scaled
        product_ref[...] = product

    outs = call(second_local, [(field, F32)] * 3 + [face_out] * nrounds)(
        *got_d, step, residual, image, inverse_here
    )
    scaled, product, part = outs[:3]
    got_e = trade(fill(outs[3:]))

    def second_coarse(
        sums_ref, table_ref, values_ref, mine_ref, image_ref, step_ref, scaled_ref, product_ref,
        first_ref, curv_ref, next_ref, values_out, inv_ref, quad_ref, work_ref
    ):
        rows = jnp.concatenate([sums_ref[k, mine : mine + nco, :] for k in range(devices)], axis=0)
        step = step_ref[...]
        values_now = values_ref[...] - dot(dot(table_ref[...], rows), step)
        values_out[...] = values_now
        own = mine_ref[0] - dot(image_ref[...], step)
        next_ref[...] = gram_dot(scaled_ref[...], product_ref[...]) + dot(own, values_now[:nco], 0, 0)
        _, on = triangles()
        inverse = solve(first_ref[...], on.astype(F32), work_ref, (), 4)
        inv_ref[...] = inverse
        quad_ref[...] = dot(inverse, deep_dot(curv_ref[...], inverse), 0, 0)

    next_part, values, first_inverse, quad = call(
        second_coarse,
        [(gram_shape, F32), ((8 * nco, cols), F32), (gram_shape, F32), (gram_shape, F32)],
        work,
        flops=2 * 12 * unknowns * cols**2,
    )(sums, table, values, coarse_input, coarse_image, step, scaled, product, first, curvature)

    per = 8 * -(-2 * cols // (8 * devices))
    blocks_out = ((devices, per, cols), F32)

    def second_direction(*refs):
        got = take(spread(refs[:nrounds]))
        part_ref, next_ref, values_ref, deep_ref, schur_ref = refs[nrounds : nrounds + 5]
        update_ref, blocks_ref = refs[nrounds + 5 :]
        update = add_faces(part_ref[...], got) + coarse_part(deep_ref[...], values_ref[...])
        update_ref[...] = update
        high = update.astype(BF16)
        low = (update - high.astype(F32)).astype(BF16)
        both = half_dot(schur_ref[...], jnp.concatenate([high, low], axis=1))
        product = both[:, :cols] + both[:, cols:]
        square = gram_dot(update, product)
        write_blocks(blocks_ref, jnp.concatenate([next_ref[...], square], axis=0))

    update, blocks = call(second_direction, [(field, F32), blocks_out])(
        *got_e, part, next_part, values, deep_bases, schur_here
    )
    blocks = lax.all_to_all(blocks, AXES, 0, 0)

    def second_sums(blocks_ref, out_ref):
        out_ref[...] = jnp.broadcast_to(jnp.sum(blocks_ref[...], axis=0)[None], out_ref.shape)

    (sums,) = call(second_sums, [blocks_out])(blocks)
    sums = lax.all_to_all(sums, AXES, 0, 0).reshape(devices * per, cols)

    def finish(
        sums_ref, inv_ref, quad_ref, step_ref, dir_ref, update_ref, out_hbm, work_ref, rows_ref, sems
    ):
        next_gram, square = sums_ref[0:cols], sums_ref[cols : 2 * cols]
        square = 0.5 * (square + square.T)
        curvature = square - dot(next_gram, deep_dot(quad_ref[...], next_gram), 0, 0)
        ratio = deep_dot(inv_ref[...], next_gram)
        step = solve(curvature, next_gram, work_ref, (1.8, 1.8, 1.5), 7)
        total = step_ref[...] + deep_dot(ratio, step)
        p, q, _ = thirds(jnp.concatenate([total, step], axis=0))
        copies = []
        for f in range(4):
            here = pl.ds(face * f, face)
            a, b, _ = thirds(jnp.concatenate([dir_ref[here], update_ref[here]], axis=1))
            rows_ref[here] = plain(a, p) + (plain(a, q) + plain(b, p))
            copies.append(
                pltpu.make_async_copy(rows_ref.at[here], out_hbm.at[here], sems.at[f])
            )
            copies[-1].start()
        for copy in copies:
            copy.wait()

    (solved,) = call(finish, [(field, F32)], work + [(field, F32)], copies=4, far_out=True)(
        sums, first_inverse, quad, step, direction, update
    )
    return solved[None, None]


def solution(mesh):
    return jax.shard_map(
        local,
        mesh=mesh,
        in_specs=(
            P("gx", "gy", None, None),
            P("gx", "gy", None, None),
            P("gx", "gy", None, None),
            P("gx", "gy", None, None),
            P("gx", "gy", None, None),
            P("gx", "gy", None),
        ),
        out_specs=P("gx", "gy", None, None),
        check_vma=False,
    )
```

```python
import jax
import jax.numpy as jnp
from jax import lax
from jax.experimental import pallas as pl
from jax.experimental.pallas import tpu as pltpu
from jax.sharding import PartitionSpec as P

AXES = ("gx", "gy")
F32 = jnp.float32
BF16 = jnp.bfloat16
EXACT = lax.Precision.HIGHEST


def dot(left, right, left_dim=1, right_dim=0, precision=EXACT):
    return lax.dot_general(
        left,
        right,
        (((left_dim,), (right_dim,)), ((), ())),
        precision=precision,
        preferred_element_type=F32,
    )


def thirds(value):
    high = value.astype(BF16)
    rest = value - high.astype(F32)
    middle = rest.astype(BF16)
    return high, middle, (rest - middle.astype(F32)).astype(BF16)


def plain(left, right, left_dim=1, right_dim=0):
    return lax.dot_general(
        left, right, (((left_dim,), (right_dim,)), ((), ())), preferred_element_type=F32
    )


def deep_dot(left, right):
    a, b, c = thirds(left)
    p, q, r = thirds(right)
    return plain(
        jnp.concatenate([a, a, b, a, c, b], axis=1), jnp.concatenate([p, q, p, r, p, q], axis=0)
    )


def gram_dot(left, right):
    a, b, _ = thirds(left)
    p, q, _ = thirds(right)
    cols = right.shape[1]
    pair = plain(a, jnp.concatenate([p, q], axis=1), 0, 0)
    return pair[:, :cols] + (pair[:, cols:] + plain(b, p, 0, 0))


def flat_dot(left, right):
    a, b, _ = thirds(left)
    p, q, _ = thirds(right)
    return plain(jnp.concatenate([a, a, b], axis=1), jnp.concatenate([p, q, p], axis=0))


def half_dot(left, right):
    return lax.dot_general(
        left, right, (((1,), (0,)), ((), ())), preferred_element_type=F32
    )


def call(body, outs, scratch=(), flops=0, moved=0, far=0, copies=0, far_outs=()):
    sems = [pltpu.SemaphoreType.DMA((copies,))] if copies else []

    def run(*args):
        specs = [pl.BlockSpec(memory_space=pltpu.HBM if i < far else pltpu.VMEM) for i in range(len(args))]
        args = [pltpu.with_memory_space_constraint(a, pltpu.HBM) if i < far else a for i, a in enumerate(args)]
        results = [
            pl.BlockSpec(memory_space=pltpu.HBM if k in far_outs else pltpu.VMEM)
            for k in range(len(outs))
        ]
        return kernel_call(body, outs, scratch, flops, moved, sems, specs, results)(*args)

    return run


def kernel_call(body, outs, scratch, flops, moved, sems, specs, results):
    return pl.pallas_call(
        body,
        in_specs=specs,
        out_specs=results,
        scratch_shapes=[pltpu.VMEM(shape, kind) for shape, kind in scratch] + sems,
        out_shape=[jax.ShapeDtypeStruct(shape, kind) for shape, kind in outs],
        compiler_params=pltpu.CompilerParams(vmem_limit_bytes=48 * 1024 * 1024),
        cost_estimate=pl.CostEstimate(flops=flops, bytes_accessed=moved, transcendentals=0),
    )


def pair_rounds(size):
    first = [(i, i + 1) for i in range(0, size - 1, 2)]
    second = [(i, i + 1) for i in range(1, size - 1, 2)]
    return [pairs + [(j, i) for i, j in pairs] for pairs in (second, first)]


def exchange(sends):
    got = []
    for axis, pieces in zip(AXES, (sends[0:2], sends[2:4])):
        for pairs, piece in zip(pair_rounds(lax.axis_size(axis)), pieces):
            got.append(lax.ppermute(piece, axis, pairs) if pairs else None)
    return got


def rounds_used():
    return [bool(p) for axis in AXES for p in pair_rounds(lax.axis_size(axis))]


def even(axis):
    return lax.rem(lax.axis_index(axis), 2) == 0


def to_rounds(faces):
    ex, ey = even("gx"), even("gy")
    return [
        jnp.where(ex, faces[0], faces[1]),
        jnp.where(ex, faces[1], faces[0]),
        jnp.where(ey, faces[2], faces[3]),
        jnp.where(ey, faces[3], faces[2]),
    ]


def to_faces(parts):
    ex, ey = even("gx"), even("gy")
    b, a, d, c = parts

    def choose(flag, yes, no):
        if yes is None and no is None:
            return None
        if yes is None:
            return jnp.where(flag, jnp.zeros_like(no), no)
        if no is None:
            return jnp.where(flag, yes, jnp.zeros_like(yes))
        return jnp.where(flag, yes, no)

    return [choose(ex, b, a), choose(ex, a, b), choose(ey, d, c), choose(ey, c, d)]


def face_weights():
    ix, iy = lax.axis_index("gx"), lax.axis_index("gy")
    shared = [
        ix > 0,
        ix < lax.axis_size("gx") - 1,
        iy > 0,
        iy < lax.axis_size("gy") - 1,
    ]
    return [jnp.where(flag, 0.5, 1.0).astype(F32) for flag in shared]


def split_faces(field):
    rows = field.shape[0] // 4
    return [field[rows * f : rows * (f + 1)] for f in range(4)]


def add_faces(field, got):
    faces = [
        mine if other is None else mine + other for mine, other in zip(split_faces(field), got)
    ]
    return jnp.concatenate(faces, axis=0)


def weighted(field, weights):
    return jnp.concatenate([w * v for w, v in zip(weights, split_faces(field))], axis=0)


def write_blocks(out_ref, rows):
    per = out_ref.shape[1]
    used = rows.shape[0] // per
    if used < out_ref.shape[0]:
        out_ref[...] = jnp.zeros(out_ref.shape, F32)
    out_ref[0:used] = rows.reshape(used, per, rows.shape[1])


def solve(matrix, right, work_ref, boosts, squarings, exact):
    size = matrix.shape[0]
    row_id = lax.broadcasted_iota(jnp.int32, (size, size), 0)
    col_id = lax.broadcasted_iota(jnp.int32, (size, size), 1)
    eye = (row_id == col_id).astype(F32)
    only = matrix * eye
    by_row = lax.rsqrt(jnp.sum(only, axis=1, keepdims=True))
    by_col = lax.rsqrt(jnp.sum(only, axis=0, keepdims=True))
    unit = matrix * by_row * by_col
    bound = jnp.max(jnp.sum(jnp.abs(unit), axis=0, keepdims=True), axis=1, keepdims=True)
    scale = 1.9 / bound
    answer = right * (by_row * scale)
    power = eye - scale * unit

    def step(answer, power, product=deep_dot):
        return answer + product(power, answer), product(power, power)

    for k in range(squarings):
        answer, power = step(answer, power, deep_dot if k < exact else flat_dot)
        if k < len(boosts):
            power = boosts[k] * power + (1.0 - boosts[k]) * eye
            answer = boosts[k] * answer

    def resume():
        work_ref[:, 0:size] = answer
        work_ref[:, size:] = power

        def again(carry):
            answer, power = step(work_ref[:, 0:size], work_ref[:, size:])
            work_ref[:, 0:size] = answer
            work_ref[:, size:] = power
            return carry[0] + 1, jnp.max(jnp.abs(power))

        lax.while_loop(
            lambda carry: jnp.logical_and(carry[0] < 40, carry[1] > 1e-7),
            again,
            (jnp.int32(0), jnp.float32(1.0)),
        )
        return work_ref[:, 0:size] * by_row

    good = jnp.sum(power * power) < 1e-4
    return (answer + deep_dot(power, answer)) * by_row, good, resume


def local(loads, schur, local_inverse, coarse_basis, coarse_inverse, face_map):
    loads, schur, local_inverse = loads[0, 0], schur[0, 0], local_inverse[0, 0]
    basis, coarse_rows, slot_map = coarse_basis[0, 0], coarse_inverse[0, 0], face_map[0, 0]
    unknowns, cols = loads.shape
    face = unknowns // 4
    nco, coarse_all = coarse_rows.shape
    devices = lax.axis_size("gx") * lax.axis_size("gy")
    chunks = coarse_all // cols
    used = rounds_used()
    field = (unknowns, cols)
    gram_shape = (cols, cols)
    work = [((cols, 2 * cols), F32)]
    face_out = ((face, cols), F32)

    def give(refs, faces):
        for ref, value, flag in zip(refs, to_rounds(faces), used):
            if flag:
                ref[...] = value

    def take(refs):
        return to_faces([ref[...] if flag else None for ref, flag in zip(refs, used)])

    def trade(sends):
        return [got for got in exchange(sends) if got is not None]

    def spread(refs):
        left = list(refs)
        return [left.pop(0) if flag else None for flag in used]

    nrounds = sum(used)

    def fill(values):
        left = list(values)
        return [left.pop(0) if flag else None for flag in used]

    head = face + nco + nco * chunks

    def send_loads(loads_hbm, basis_hbm, rows_hbm, map_hbm, loads_ref, basis_ref, rows_ref, map_ref, *outs):
        outs, raw_ref, sems = spread(outs[:-2]), outs[-2], outs[-1]
        fetches = [
            pltpu.make_async_copy(src, dst, sems.at[k])
            for k, (src, dst) in enumerate(
                ((loads_hbm, raw_ref), (basis_hbm, basis_ref), (rows_hbm, rows_ref), (map_hbm, map_ref))
            )
        ]
        for fetch in fetches:
            fetch.start()
        for fetch in fetches:
            fetch.wait()
        wide_loads = raw_ref[...].astype(F32)
        loads_ref[...] = wide_loads
        basis_now = basis_ref[...]
        rows_now = rows_ref[...]
        packs = []
        for f, part in enumerate(split_faces(wide_loads)):
            packs.append(
                jnp.concatenate(
                    [part, basis_now[:, face * f : face * (f + 1)]]
                    + [rows_now[:, cols * c : cols * (c + 1)] for c in range(chunks)],
                    axis=0,
                )
            )
        give(outs, packs)

    outs = call(
        send_loads,
        [(field, F32), (basis.shape, F32), (coarse_rows.shape, F32), ((1, unknowns), jnp.int32)]
        + [((head, cols), F32)] * nrounds,
        [(field, BF16)],
        far=4,
        copies=4,
    )(loads, basis, coarse_rows, slot_map.reshape(1, unknowns))
    loads, basis, coarse_rows, slot_map = outs[:4]
    got_a = trade(fill(outs[4:]))

    square = (unknowns, unknowns)

    def reorder(first_hbm, second_hbm, map_ref, first_out, second_out, first_raw, second_raw, sems):
        fetches = [
            pltpu.make_async_copy(src, dst, sems.at[k])
            for k, (src, dst) in enumerate(((first_hbm, first_raw), (second_hbm, second_raw)))
        ]
        for fetch in fetches:
            fetch.start()
        slots = lax.broadcasted_iota(jnp.int32, square, 0)
        pick = (slots == map_ref[...]).astype(F32).astype(BF16)
        for fetch, ref, out in zip(fetches, (first_raw, second_raw), (first_out, second_out)):
            fetch.wait()
            rows = half_dot(pick, ref[...]).astype(BF16)
            out[...] = plain(rows, pick, 1, 1).astype(BF16)

    inverse_here, schur_here = call(
        reorder,
        [(square, BF16)] * 2,
        [(square, BF16)] * 2,
        flops=8 * unknowns**3,
        moved=8 * unknowns**2,
        far=2,
        copies=2,
    )(local_inverse, schur, slot_map)

    def first_local(*refs):
        got = take(spread(refs[:nrounds]))
        loads_ref, inverse_ref, basis_ref = refs[nrounds : nrounds + 3]
        res_ref, scaled_ref, product_ref, part_ref, mine_ref, ci_hbm = refs[nrounds + 3 : nrounds + 9]
        sends, ci_ref, sems = spread(refs[nrounds + 9 : -2]), refs[-2], refs[-1]
        weights = face_weights()
        residual = add_faces(loads_ref[...], [g if g is None else g[:face] for g in got])
        scaled = weighted(residual, weights)
        coarse_input = dot(basis_ref[...], scaled)
        mine_ref[...] = coarse_input
        ci_ref[...] = jnp.broadcast_to(coarse_input[None], ci_ref.shape)
        copy = pltpu.make_async_copy(ci_ref, ci_hbm, sems.at[0])
        copy.start()
        product = half_dot(inverse_ref[...], scaled.astype(BF16))
        part = weighted(product, weights)
        give(sends, split_faces(part))
        res_ref[...] = residual
        scaled_ref[...] = scaled
        product_ref[...] = product
        part_ref[...] = part
        copy.wait()

    spread_rows = ((devices, nco, cols), F32)
    outs = call(
        first_local,
        [(field, F32)] * 4 + [((nco, cols), F32), spread_rows] + [face_out] * nrounds,
        [spread_rows],
        copies=1,
        far_outs=(5,),
    )(*got_a, loads, inverse_here, basis)
    residual, scaled, product, part, coarse_mine, coarse_input = outs[:6]
    got_b = trade(fill(outs[6:]))
    coarse_all_in = lax.all_to_all(coarse_input, AXES, 0, 0).reshape(coarse_all, cols)

    def first_tables(*refs):
        got = take(spread(refs[:nrounds]))
        scaled_ref, product_ref, basis_ref, rows_ref = refs[nrounds : nrounds + 4]
        gram_ref, bases_ref, deep_ref, table_ref = refs[nrounds + 4 :]
        weights = face_weights()
        gram_ref[...] = gram_dot(scaled_ref[...], product_ref[...])
        basis_now = basis_ref[...]
        bases, tables = [], []
        for f in range(4):
            mine_now = weights[f] * basis_now[:, face * f : face * (f + 1)]
            other = got[f]
            if other is None:
                both = [mine_now, jnp.zeros_like(mine_now)]
                tables += [rows_ref[...], jnp.zeros((nco, coarse_all), F32)]
            else:
                both = [mine_now, 0.5 * other[face : face + nco]]
                tables += [
                    rows_ref[...],
                    jnp.concatenate(
                        [
                            other[face + nco * (c + 1) : face + nco * (c + 2)]
                            for c in range(chunks)
                        ],
                        axis=1,
                    ),
                ]
            none = jnp.zeros((2 * nco, face), F32)
            block = jnp.concatenate(both, axis=0)
            bases.append(jnp.concatenate([block if k == f else none for k in range(4)], axis=1))
        by_row = jnp.concatenate(bases, axis=0).T
        bases_ref[...] = by_row
        a, b, c = thirds(by_row)
        deep_ref[...] = jnp.concatenate([a, a, b, a, c, b], axis=1)
        table_ref[...] = jnp.concatenate(tables, axis=0)

    gram_part, bases, deep_bases, table = call(
        first_tables,
        [
            (gram_shape, F32),
            ((unknowns, 8 * nco), F32),
            ((unknowns, 48 * nco), BF16),
            ((8 * nco, coarse_all), F32),
        ],
    )(*got_a, scaled, product, basis, coarse_rows)

    def coarse_part(deep, values):
        p, q, r = thirds(values)
        return plain(deep, jnp.concatenate([p, q, p, r, p, q], axis=0))

    mine = -(-cols // devices)
    packers = cols // mine
    tall = max(mine, nco)
    block_shape = (devices, 3, tall, cols)

    def identity():
        row_id = lax.broadcasted_iota(jnp.int32, gram_shape, 0)
        col_id = lax.broadcasted_iota(jnp.int32, gram_shape, 1)
        return (row_id == col_id).astype(F32)

    def first_coarse(all_ref, deep_ref, table_ref, mine_ref, gram_ref, values_ref, coarse_ref, first_ref):
        values = deep_dot(table_ref[...], all_ref[...])
        values_ref[...] = values
        coarse_ref[...] = coarse_part(deep_ref[...], values)
        rows, results = mine_ref[...], values[:nco]
        first_ref[...] = gram_ref[...] + dot(rows, results, 0, 0)

    values, coarse, first_part = call(
        first_coarse, [((8 * nco, cols), F32), (field, F32), (gram_shape, F32)]
    )(coarse_all_in, deep_bases, table, coarse_mine, gram_part)

    def first_direction(*refs):
        got = take(spread(refs[:nrounds]))
        part_ref, coarse_ref, bases_ref, schur_ref, first_ref = refs[nrounds : nrounds + 5]
        dir_ref, image_ref, blocks_ref = refs[nrounds + 5 : nrounds + 8]
        sends = spread(refs[nrounds + 8 :])
        if packers < devices or mine < tall:
            blocks_ref[...] = jnp.zeros(blocks_ref.shape, F32)
        else:
            blocks_ref[:, 2] = jnp.zeros((devices, tall, cols), F32)
        update = add_faces(part_ref[...], got) + coarse_ref[...]
        dir_ref[...] = update
        image = half_dot(schur_ref[...], update.astype(BF16))
        image_ref[...] = image
        give(sends, split_faces(image))
        stack = gram_dot(jnp.concatenate([update, bases_ref[...]], axis=1), image)
        curvature, shares = stack[:cols], stack[cols:]
        for at, gram in ((0, curvature), (1, first_ref[...])):
            for k in range(packers):
                blocks_ref[k, at, 0:mine] = gram[mine * k : mine * (k + 1)]
        ix, iy = lax.axis_index("gx"), lax.axis_index("gy")
        sx, sy = lax.axis_size("gx"), lax.axis_size("gy")
        own = shares[0:nco]
        for f in range(1, 4):
            own = own + shares[2 * nco * f : 2 * nco * f + nco]
        here = ix * sy + iy
        targets = [
            (here, own, None),
            (here - sy, shares[nco : 2 * nco], ix > 0),
            (here + sy, shares[3 * nco : 4 * nco], ix < sx - 1),
            (here - 1, shares[5 * nco : 6 * nco], iy > 0),
            (here + 1, shares[7 * nco : 8 * nco], iy < sy - 1),
        ]

        def put(target, rows):
            blocks_ref[target, 2, 0:nco] = rows

        for target, rows, flag in targets:
            if flag is None:
                put(target, rows)
            else:
                pl.when(flag)(lambda target=target, rows=rows: put(target, rows))

    outs = call(
        first_direction,
        [(field, F32), (field, F32), (block_shape, F32)] + [face_out] * nrounds,
    )(*got_b, part, coarse, bases, schur_here, first_part)
    direction, image, blocks = outs[:3]
    got_d = trade(fill(outs[3:]))
    blocks = lax.all_to_all(blocks, AXES, 0, 0)

    groups = 4 if devices % 4 == 0 else 1

    def first_sums(blocks_ref, sum_hbm, mine_ref, sum_ref, sems):
        total = jnp.sum(blocks_ref[...], axis=0)
        mine_ref[...] = total[2, 0:nco]
        sum_ref[...] = jnp.broadcast_to(total[None], sum_ref.shape)
        copies = [
            pltpu.make_async_copy(
                sum_ref, sum_hbm.at[pl.ds(devices // groups * k, devices // groups)], sems.at[k]
            )
            for k in range(groups)
        ]
        for copy in copies:
            copy.start()
        for copy in copies:
            copy.wait()

    sums, coarse_image = call(
        first_sums,
        [(block_shape, F32), ((nco, cols), F32)],
        [((devices // groups, 3, tall, cols), F32)],
        copies=groups,
        far_outs=(0,),
    )(blocks)
    sums = lax.all_to_all(sums, AXES, 0, 0)

    def gathered(ref, at, rows, blocks):
        return jnp.concatenate([ref[k, at, 0:rows] for k in range(blocks)], axis=0)

    def first_step(sums_ref, raw_ref, curv_ref, first_ref, step_ref, work_ref):
        raw = gathered(sums_ref, 0, mine, packers)
        curvature = 0.5 * (raw + raw.T)
        first = gathered(sums_ref, 1, mine, packers)
        raw_ref[...] = raw
        curv_ref[...] = curvature
        first_ref[...] = first
        step, good, resume = solve(curvature, first, work_ref, (1.33,), 4, 2)
        step_ref[...] = step

        @pl.when(jnp.logical_not(good))
        def _():
            step_ref[...] = resume()

    raw_curvature, curvature, first, step = call(first_step, [(gram_shape, F32)] * 4, work, flops=2 * 12 * cols**3)(
        sums
    )

    def second_local(*refs):
        got = take(spread(refs[:nrounds]))
        step_ref, res_ref, image_ref, inverse_ref = refs[nrounds : nrounds + 4]
        scaled_ref, product_ref, part_ref = refs[nrounds + 4 : nrounds + 7]
        sends = spread(refs[nrounds + 7 :])
        weights = face_weights()
        residual = res_ref[...] - dot(add_faces(image_ref[...], got), step_ref[...])
        scaled = weighted(residual, weights)
        product = half_dot(inverse_ref[...], scaled.astype(BF16))
        part = weighted(product, weights)
        part_ref[...] = part
        give(sends, split_faces(part))
        scaled_ref[...] = scaled
        product_ref[...] = product

    outs = call(second_local, [(field, F32)] * 3 + [face_out] * nrounds)(
        *got_d, step, residual, image, inverse_here
    )
    scaled, product, part = outs[:3]
    got_e = trade(fill(outs[3:]))

    def second_coarse(
        sums_ref, table_ref, values_ref, mine_ref, image_ref, step_ref, scaled_ref, product_ref,
        first_ref, curv_ref, raw_ref, next_ref, values_out, inv_ref, quad_ref, mend_ref, work_ref
    ):
        rows = gathered(sums_ref, 2, nco, devices)
        step = step_ref[...]
        values_now = values_ref[...] - dot(dot(table_ref[...], rows), step)
        values_out[...] = values_now
        own = mine_ref[...] - dot(image_ref[...], step)
        next_ref[...] = gram_dot(scaled_ref[...], product_ref[...]) + dot(own, values_now[:nco], 0, 0)
        first, curvature = first_ref[...], curv_ref[...]
        mend_ref[...] = 2.0 * (first.T - deep_dot(raw_ref[...], step))
        inverse, good, resume = solve(0.5 * (first + first.T), identity(), work_ref, (), 4, 1)

        def keep(inverse):
            inv_ref[...] = inverse
            quad_ref[...] = deep_dot(deep_dot(inverse, curvature), inverse)

        keep(inverse)

        @pl.when(jnp.logical_not(good))
        def _():
            keep(resume())

    next_part, values, first_inverse, quad, mend = call(
        second_coarse,
        [(gram_shape, F32), ((8 * nco, cols), F32)] + [(gram_shape, F32)] * 3,
        work,
        flops=2 * 12 * unknowns * cols**2,
    )(sums, table, values, coarse_mine, coarse_image, step, scaled, product, first, curvature, raw_curvature)

    per = 8 * -(-2 * cols // (8 * devices))
    blocks_out = ((devices, per, cols), F32)

    def second_direction(*refs):
        got = take(spread(refs[:nrounds]))
        part_ref, next_ref, values_ref, deep_ref, schur_ref = refs[nrounds : nrounds + 5]
        update_ref, blocks_ref = refs[nrounds + 5 :]
        update = add_faces(part_ref[...], got) + coarse_part(deep_ref[...], values_ref[...])
        update_ref[...] = update
        high = update.astype(BF16)
        low = (update - high.astype(F32)).astype(BF16)
        both = half_dot(schur_ref[...], jnp.concatenate([high, low], axis=1))
        product = both[:, :cols] + both[:, cols:]
        square = gram_dot(update, product)
        write_blocks(blocks_ref, jnp.concatenate([next_ref[...], square], axis=0))

    update, blocks = call(second_direction, [(field, F32), blocks_out])(
        *got_e, part, next_part, values, deep_bases, schur_here
    )
    blocks = lax.all_to_all(blocks, AXES, 0, 0)

    def second_sums(blocks_ref, out_ref):
        out_ref[...] = jnp.broadcast_to(jnp.sum(blocks_ref[...], axis=0)[None], out_ref.shape)

    (sums,) = call(second_sums, [blocks_out])(blocks)
    sums = lax.all_to_all(sums, AXES, 0, 0).reshape(devices * per, cols)

    def finish(
        sums_ref, inv_ref, quad_ref, mend_ref, step_ref, dir_ref, update_ref, out_ref, work_ref
    ):
        next_gram, square = sums_ref[0:cols], sums_ref[cols : 2 * cols]
        ratio = deep_dot(inv_ref[...], next_gram)
        reduced = square - dot(next_gram, deep_dot(quad_ref[...], next_gram - mend_ref[...]), 0, 0)
        curvature = 0.5 * (reduced + reduced.T)
        step, good, resume = solve(curvature, next_gram, work_ref, (1.8, 1.8, 1.5, 1.14), 6, 2)

        def write(step):
            total = step_ref[...] + deep_dot(ratio, step)
            p, q, _ = thirds(jnp.concatenate([total, step], axis=0))
            a, b, _ = thirds(jnp.concatenate([dir_ref[...], update_ref[...]], axis=1))
            pair = plain(a, jnp.concatenate([p, q], axis=1))
            out_ref[...] = pair[:, :cols] + (pair[:, cols:] + plain(b, p))

        write(step)

        @pl.when(jnp.logical_not(good))
        def _():
            write(resume())

    (solved,) = call(finish, [(field, F32)], work)(
        sums, first_inverse, quad, mend, step, direction, update
    )
    return solved[None, None]


def solution(mesh):
    return jax.shard_map(
        local,
        mesh=mesh,
        in_specs=(
            P("gx", "gy", None, None),
            P("gx", "gy", None, None),
            P("gx", "gy", None, None),
            P("gx", "gy", None, None),
            P("gx", "gy", None, None),
            P("gx", "gy", None),
        ),
        out_specs=P("gx", "gy", None, None),
        check_vma=False,
    )
```

```python
import jax
import jax.numpy as jnp
from jax import lax
from jax.experimental import pallas as pl
from jax.experimental.pallas import tpu as pltpu
from jax.sharding import PartitionSpec as P

AXES = ("gx", "gy")
F32 = jnp.float32
BF16 = jnp.bfloat16
EXACT = lax.Precision.HIGHEST


def dot(left, right, left_dim=1, right_dim=0, precision=EXACT):
    return lax.dot_general(
        left,
        right,
        (((left_dim,), (right_dim,)), ((), ())),
        precision=precision,
        preferred_element_type=F32,
    )


def thirds(value):
    high = value.astype(BF16)
    rest = value - high.astype(F32)
    middle = rest.astype(BF16)
    return high, middle, (rest - middle.astype(F32)).astype(BF16)


def plain(left, right, left_dim=1, right_dim=0):
    return lax.dot_general(
        left, right, (((left_dim,), (right_dim,)), ((), ())), preferred_element_type=F32
    )


def deep_dot(left, right):
    a, b, c = thirds(left)
    p, q, r = thirds(right)
    return plain(
        jnp.concatenate([a, a, b, a, c, b], axis=1), jnp.concatenate([p, q, p, r, p, q], axis=0)
    )


def gram_dot(left, right):
    a, b, _ = thirds(left)
    p, q, _ = thirds(right)
    cols = right.shape[1]
    pair = plain(a, jnp.concatenate([p, q], axis=1), 0, 0)
    return pair[:, :cols] + (pair[:, cols:] + plain(b, p, 0, 0))


def flat_dot(left, right):
    a, b, _ = thirds(left)
    p, q, _ = thirds(right)
    return plain(jnp.concatenate([a, a, b], axis=1), jnp.concatenate([p, q, p], axis=0))


def half_dot(left, right):
    return lax.dot_general(
        left, right, (((1,), (0,)), ((), ())), preferred_element_type=F32
    )


def call(body, outs, scratch=(), flops=0, moved=0, far=0, copies=0, far_outs=()):
    sems = [pltpu.SemaphoreType.DMA((copies,))] if copies else []

    def run(*args):
        specs = [pl.BlockSpec(memory_space=pltpu.HBM if i < far else pltpu.VMEM) for i in range(len(args))]
        args = [pltpu.with_memory_space_constraint(a, pltpu.HBM) if i < far else a for i, a in enumerate(args)]
        results = [
            pl.BlockSpec(memory_space=pltpu.HBM if k in far_outs else pltpu.VMEM)
            for k in range(len(outs))
        ]
        return kernel_call(body, outs, scratch, flops, moved, sems, specs, results)(*args)

    return run


def kernel_call(body, outs, scratch, flops, moved, sems, specs, results):
    return pl.pallas_call(
        body,
        in_specs=specs,
        out_specs=results,
        scratch_shapes=[pltpu.VMEM(shape, kind) for shape, kind in scratch] + sems,
        out_shape=[jax.ShapeDtypeStruct(shape, kind) for shape, kind in outs],
        compiler_params=pltpu.CompilerParams(vmem_limit_bytes=48 * 1024 * 1024),
        cost_estimate=pl.CostEstimate(flops=flops, bytes_accessed=moved, transcendentals=0),
    )


def pair_rounds(size):
    first = [(i, i + 1) for i in range(0, size - 1, 2)]
    second = [(i, i + 1) for i in range(1, size - 1, 2)]
    return [pairs + [(j, i) for i, j in pairs] for pairs in (second, first)]


def exchange(sends):
    got = []
    for axis, pieces in zip(AXES, (sends[0:2], sends[2:4])):
        for pairs, piece in zip(pair_rounds(lax.axis_size(axis)), pieces):
            got.append(lax.ppermute(piece, axis, pairs) if pairs else None)
    return got


def rounds_used():
    return [bool(p) for axis in AXES for p in pair_rounds(lax.axis_size(axis))]


def even(axis):
    return lax.rem(lax.axis_index(axis), 2) == 0


def to_rounds(faces):
    ex, ey = even("gx"), even("gy")
    return [
        jnp.where(ex, faces[0], faces[1]),
        jnp.where(ex, faces[1], faces[0]),
        jnp.where(ey, faces[2], faces[3]),
        jnp.where(ey, faces[3], faces[2]),
    ]


def to_faces(parts):
    ex, ey = even("gx"), even("gy")
    b, a, d, c = parts

    def choose(flag, yes, no):
        if yes is None and no is None:
            return None
        if yes is None:
            return jnp.where(flag, jnp.zeros_like(no), no)
        if no is None:
            return jnp.where(flag, yes, jnp.zeros_like(yes))
        return jnp.where(flag, yes, no)

    return [choose(ex, b, a), choose(ex, a, b), choose(ey, d, c), choose(ey, c, d)]


def face_weights():
    ix, iy = lax.axis_index("gx"), lax.axis_index("gy")
    shared = [
        ix > 0,
        ix < lax.axis_size("gx") - 1,
        iy > 0,
        iy < lax.axis_size("gy") - 1,
    ]
    return [jnp.where(flag, 0.5, 1.0).astype(F32) for flag in shared]


def split_faces(field):
    rows = field.shape[0] // 4
    return [field[rows * f : rows * (f + 1)] for f in range(4)]


def add_faces(field, got):
    faces = [
        mine if other is None else mine + other for mine, other in zip(split_faces(field), got)
    ]
    return jnp.concatenate(faces, axis=0)


def weighted(field, weights):
    return jnp.concatenate([w * v for w, v in zip(weights, split_faces(field))], axis=0)


def write_blocks(out_ref, rows):
    per = out_ref.shape[1]
    used = rows.shape[0] // per
    if used < out_ref.shape[0]:
        out_ref[...] = jnp.zeros(out_ref.shape, F32)
    out_ref[0:used] = rows.reshape(used, per, rows.shape[1])


def solve(matrix, right, work_ref, boosts, squarings, exact):
    size = matrix.shape[0]
    row_id = lax.broadcasted_iota(jnp.int32, (size, size), 0)
    col_id = lax.broadcasted_iota(jnp.int32, (size, size), 1)
    eye = (row_id == col_id).astype(F32)
    only = matrix * eye
    by_row = lax.rsqrt(jnp.sum(only, axis=1, keepdims=True))
    by_col = lax.rsqrt(jnp.sum(only, axis=0, keepdims=True))
    unit = matrix * by_row * by_col
    bound = jnp.max(jnp.sum(jnp.abs(unit), axis=0, keepdims=True), axis=1, keepdims=True)
    scale = 1.9 / bound
    right = right * by_row
    answer = right * scale
    power = eye - scale * unit

    def step(answer, power, product=deep_dot):
        return answer + product(power, answer), product(power, power)

    for k in range(squarings):
        answer, power = step(answer, power, deep_dot if k < exact else flat_dot)
        if k < len(boosts):
            power = boosts[k] * power + (1.0 - boosts[k]) * eye
            answer = boosts[k] * answer

    def resume():
        work_ref[:, 2 * size :] = jnp.zeros((size, size), F32)

        def again(carry):
            answer, power = step(work_ref[:, 0:size], work_ref[:, size : 2 * size])
            work_ref[:, 0:size] = answer
            work_ref[:, size : 2 * size] = power
            return carry[0] + 1, jnp.max(jnp.abs(power))

        def refine(_, carry):
            work_ref[:, 0:size] = (right - deep_dot(unit, work_ref[:, 2 * size :])) * scale
            work_ref[:, size : 2 * size] = eye - scale * unit
            lax.while_loop(
                lambda carry: jnp.logical_and(carry[0] < 40, carry[1] > 1e-7),
                again,
                (jnp.int32(0), jnp.float32(1.0)),
            )
            work_ref[:, 2 * size :] = work_ref[:, 2 * size :] + work_ref[:, 0:size]
            return carry

        lax.fori_loop(0, 3, refine, jnp.int32(0))
        return work_ref[:, 2 * size :] * by_row

    good = jnp.sum(power * power) < 1e-4
    return (answer + deep_dot(power, answer)) * by_row, good, resume


def local(loads, schur, local_inverse, coarse_basis, coarse_inverse, face_map):
    loads, schur, local_inverse = loads[0, 0], schur[0, 0], local_inverse[0, 0]
    basis, coarse_rows, slot_map = coarse_basis[0, 0], coarse_inverse[0, 0], face_map[0, 0]
    unknowns, cols = loads.shape
    face = unknowns // 4
    nco, coarse_all = coarse_rows.shape
    devices = lax.axis_size("gx") * lax.axis_size("gy")
    chunks = coarse_all // cols
    used = rounds_used()
    field = (unknowns, cols)
    gram_shape = (cols, cols)
    work = [((cols, 3 * cols), F32)]
    face_out = ((face, cols), F32)

    def give(refs, faces):
        for ref, value, flag in zip(refs, to_rounds(faces), used):
            if flag:
                ref[...] = value

    def take(refs):
        return to_faces([ref[...] if flag else None for ref, flag in zip(refs, used)])

    def trade(sends):
        return [got for got in exchange(sends) if got is not None]

    def spread(refs):
        left = list(refs)
        return [left.pop(0) if flag else None for flag in used]

    nrounds = sum(used)

    def fill(values):
        left = list(values)
        return [left.pop(0) if flag else None for flag in used]

    head = face + nco + nco * chunks

    def send_loads(loads_hbm, basis_hbm, rows_hbm, map_hbm, loads_ref, basis_ref, rows_ref, map_ref, *outs):
        outs, raw_ref, sems = spread(outs[:-2]), outs[-2], outs[-1]
        fetches = [
            pltpu.make_async_copy(src, dst, sems.at[k])
            for k, (src, dst) in enumerate(
                ((loads_hbm, raw_ref), (basis_hbm, basis_ref), (rows_hbm, rows_ref), (map_hbm, map_ref))
            )
        ]
        for fetch in fetches:
            fetch.start()
        for fetch in fetches:
            fetch.wait()
        wide_loads = raw_ref[...].astype(F32)
        loads_ref[...] = wide_loads
        basis_now = basis_ref[...]
        rows_now = rows_ref[...]
        packs = []
        for f, part in enumerate(split_faces(wide_loads)):
            packs.append(
                jnp.concatenate(
                    [part, basis_now[:, face * f : face * (f + 1)]]
                    + [rows_now[:, cols * c : cols * (c + 1)] for c in range(chunks)],
                    axis=0,
                )
            )
        give(outs, packs)

    outs = call(
        send_loads,
        [(field, F32), (basis.shape, F32), (coarse_rows.shape, F32), ((1, unknowns), jnp.int32)]
        + [((head, cols), F32)] * nrounds,
        [(field, BF16)],
        far=4,
        copies=4,
    )(loads, basis, coarse_rows, slot_map.reshape(1, unknowns))
    loads, basis, coarse_rows, slot_map = outs[:4]
    got_a = trade(fill(outs[4:]))

    square = (unknowns, unknowns)

    def reorder(first_hbm, second_hbm, map_ref, first_out, second_out, first_raw, second_raw, sems):
        fetches = [
            pltpu.make_async_copy(src, dst, sems.at[k])
            for k, (src, dst) in enumerate(((first_hbm, first_raw), (second_hbm, second_raw)))
        ]
        for fetch in fetches:
            fetch.start()
        slots = lax.broadcasted_iota(jnp.int32, square, 0)
        pick = (slots == map_ref[...]).astype(F32).astype(BF16)
        for fetch, ref, out in zip(fetches, (first_raw, second_raw), (first_out, second_out)):
            fetch.wait()
            rows = half_dot(pick, ref[...]).astype(BF16)
            out[...] = plain(rows, pick, 1, 1).astype(BF16)

    inverse_here, schur_here = call(
        reorder,
        [(square, BF16)] * 2,
        [(square, BF16)] * 2,
        flops=8 * unknowns**3,
        moved=8 * unknowns**2,
        far=2,
        copies=2,
    )(local_inverse, schur, slot_map)

    def first_local(*refs):
        got = take(spread(refs[:nrounds]))
        loads_ref, inverse_ref, basis_ref = refs[nrounds : nrounds + 3]
        res_ref, scaled_ref, product_ref, part_ref, mine_ref, ci_hbm = refs[nrounds + 3 : nrounds + 9]
        sends, ci_ref, sems = spread(refs[nrounds + 9 : -2]), refs[-2], refs[-1]
        weights = face_weights()
        residual = add_faces(loads_ref[...], [g if g is None else g[:face] for g in got])
        scaled = weighted(residual, weights)
        coarse_input = dot(basis_ref[...], scaled)
        mine_ref[...] = coarse_input
        ci_ref[...] = jnp.broadcast_to(coarse_input[None], ci_ref.shape)
        copy = pltpu.make_async_copy(ci_ref, ci_hbm, sems.at[0])
        copy.start()
        product = half_dot(inverse_ref[...], scaled.astype(BF16))
        part = weighted(product, weights)
        give(sends, split_faces(part))
        res_ref[...] = residual
        scaled_ref[...] = scaled
        product_ref[...] = product
        part_ref[...] = part
        copy.wait()

    spread_rows = ((devices, nco, cols), F32)
    outs = call(
        first_local,
        [(field, F32)] * 4 + [((nco, cols), F32), spread_rows] + [face_out] * nrounds,
        [spread_rows],
        copies=1,
        far_outs=(5,),
    )(*got_a, loads, inverse_here, basis)
    residual, scaled, product, part, coarse_mine, coarse_input = outs[:6]
    got_b = trade(fill(outs[6:]))
    coarse_all_in = lax.all_to_all(coarse_input, AXES, 0, 0).reshape(coarse_all, cols)

    def first_tables(*refs):
        got = take(spread(refs[:nrounds]))
        scaled_ref, product_ref, basis_ref, rows_ref = refs[nrounds : nrounds + 4]
        gram_ref, bases_ref, deep_ref, table_ref = refs[nrounds + 4 :]
        weights = face_weights()
        gram_ref[...] = gram_dot(scaled_ref[...], product_ref[...])
        basis_now = basis_ref[...]
        bases, tables = [], []
        for f in range(4):
            mine_now = weights[f] * basis_now[:, face * f : face * (f + 1)]
            other = got[f]
            if other is None:
                both = [mine_now, jnp.zeros_like(mine_now)]
                tables += [rows_ref[...], jnp.zeros((nco, coarse_all), F32)]
            else:
                both = [mine_now, 0.5 * other[face : face + nco]]
                tables += [
                    rows_ref[...],
                    jnp.concatenate(
                        [
                            other[face + nco * (c + 1) : face + nco * (c + 2)]
                            for c in range(chunks)
                        ],
                        axis=1,
                    ),
                ]
            none = jnp.zeros((2 * nco, face), F32)
            block = jnp.concatenate(both, axis=0)
            bases.append(jnp.concatenate([block if k == f else none for k in range(4)], axis=1))
        by_row = jnp.concatenate(bases, axis=0).T
        bases_ref[...] = by_row
        a, b, c = thirds(by_row)
        deep_ref[...] = jnp.concatenate([a, a, b, a, c, b], axis=1)
        table_ref[...] = jnp.concatenate(tables, axis=0)

    gram_part, bases, deep_bases, table = call(
        first_tables,
        [
            (gram_shape, F32),
            ((unknowns, 8 * nco), F32),
            ((unknowns, 48 * nco), BF16),
            ((8 * nco, coarse_all), F32),
        ],
    )(*got_a, scaled, product, basis, coarse_rows)

    def coarse_part(deep, values):
        p, q, r = thirds(values)
        return plain(deep, jnp.concatenate([p, q, p, r, p, q], axis=0))

    mine = -(-cols // devices)
    packers = cols // mine
    tall = max(mine, nco)
    block_shape = (devices, 3, tall, cols)

    def identity():
        row_id = lax.broadcasted_iota(jnp.int32, gram_shape, 0)
        col_id = lax.broadcasted_iota(jnp.int32, gram_shape, 1)
        return (row_id == col_id).astype(F32)

    def first_coarse(all_ref, deep_ref, table_ref, mine_ref, gram_ref, values_ref, coarse_ref, first_ref):
        values = deep_dot(table_ref[...], all_ref[...])
        values_ref[...] = values
        coarse_ref[...] = coarse_part(deep_ref[...], values)
        rows, results = mine_ref[...], values[:nco]
        first_ref[...] = gram_ref[...] + dot(rows, results, 0, 0)

    values, coarse, first_part = call(
        first_coarse, [((8 * nco, cols), F32), (field, F32), (gram_shape, F32)]
    )(coarse_all_in, deep_bases, table, coarse_mine, gram_part)

    def first_direction(*refs):
        got = take(spread(refs[:nrounds]))
        part_ref, coarse_ref, bases_ref, schur_ref, first_ref = refs[nrounds : nrounds + 5]
        dir_ref, image_ref, blocks_ref = refs[nrounds + 5 : nrounds + 8]
        sends = spread(refs[nrounds + 8 :])
        if packers < devices or mine < tall:
            blocks_ref[...] = jnp.zeros(blocks_ref.shape, F32)
        else:
            blocks_ref[:, 2] = jnp.zeros((devices, tall, cols), F32)
        update = add_faces(part_ref[...], got) + coarse_ref[...]
        dir_ref[...] = update
        image = half_dot(schur_ref[...], update.astype(BF16))
        image_ref[...] = image
        give(sends, split_faces(image))
        stack = gram_dot(jnp.concatenate([update, bases_ref[...]], axis=1), image)
        curvature, shares = stack[:cols], stack[cols:]
        for at, gram in ((0, curvature), (1, first_ref[...])):
            for k in range(packers):
                blocks_ref[k, at, 0:mine] = gram[mine * k : mine * (k + 1)]
        ix, iy = lax.axis_index("gx"), lax.axis_index("gy")
        sx, sy = lax.axis_size("gx"), lax.axis_size("gy")
        own = shares[0:nco]
        for f in range(1, 4):
            own = own + shares[2 * nco * f : 2 * nco * f + nco]
        here = ix * sy + iy
        targets = [
            (here, own, None),
            (here - sy, shares[nco : 2 * nco], ix > 0),
            (here + sy, shares[3 * nco : 4 * nco], ix < sx - 1),
            (here - 1, shares[5 * nco : 6 * nco], iy > 0),
            (here + 1, shares[7 * nco : 8 * nco], iy < sy - 1),
        ]

        def put(target, rows):
            blocks_ref[target, 2, 0:nco] = rows

        for target, rows, flag in targets:
            if flag is None:
                put(target, rows)
            else:
                pl.when(flag)(lambda target=target, rows=rows: put(target, rows))

    outs = call(
        first_direction,
        [(field, F32), (field, F32), (block_shape, F32)] + [face_out] * nrounds,
    )(*got_b, part, coarse, bases, schur_here, first_part)
    direction, image, blocks = outs[:3]
    got_d = trade(fill(outs[3:]))
    blocks = lax.all_to_all(blocks, AXES, 0, 0)

    groups = 4 if devices % 4 == 0 else 1

    def first_sums(blocks_ref, sum_hbm, mine_ref, sum_ref, sems):
        total = jnp.sum(blocks_ref[...], axis=0)
        mine_ref[...] = total[2, 0:nco]
        sum_ref[...] = jnp.broadcast_to(total[None], sum_ref.shape)
        copies = [
            pltpu.make_async_copy(
                sum_ref, sum_hbm.at[pl.ds(devices // groups * k, devices // groups)], sems.at[k]
            )
            for k in range(groups)
        ]
        for copy in copies:
            copy.start()
        for copy in copies:
            copy.wait()

    sums, coarse_image = call(
        first_sums,
        [(block_shape, F32), ((nco, cols), F32)],
        [((devices // groups, 3, tall, cols), F32)],
        copies=groups,
        far_outs=(0,),
    )(blocks)
    sums = lax.all_to_all(sums, AXES, 0, 0)

    def gathered(ref, at, rows, blocks):
        return jnp.concatenate([ref[k, at, 0:rows] for k in range(blocks)], axis=0)

    def first_step(sums_ref, raw_ref, curv_ref, first_ref, step_ref, work_ref):
        raw = gathered(sums_ref, 0, mine, packers)
        curvature = 0.5 * (raw + raw.T)
        first = gathered(sums_ref, 1, mine, packers)
        raw_ref[...] = raw
        curv_ref[...] = curvature
        first_ref[...] = first
        step, good, resume = solve(curvature, first, work_ref, (1.33,), 4, 4)
        step_ref[...] = step

        @pl.when(jnp.logical_not(good))
        def _():
            step_ref[...] = resume()

    raw_curvature, curvature, first, step = call(first_step, [(gram_shape, F32)] * 4, work, flops=2 * 12 * cols**3)(
        sums
    )

    def second_local(*refs):
        got = take(spread(refs[:nrounds]))
        step_ref, res_ref, image_ref, inverse_ref = refs[nrounds : nrounds + 4]
        scaled_ref, product_ref, part_ref = refs[nrounds + 4 : nrounds + 7]
        sends = spread(refs[nrounds + 7 :])
        weights = face_weights()
        residual = res_ref[...] - dot(add_faces(image_ref[...], got), step_ref[...])
        scaled = weighted(residual, weights)
        product = half_dot(inverse_ref[...], scaled.astype(BF16))
        part = weighted(product, weights)
        part_ref[...] = part
        give(sends, split_faces(part))
        scaled_ref[...] = scaled
        product_ref[...] = product

    outs = call(second_local, [(field, F32)] * 3 + [face_out] * nrounds)(
        *got_d, step, residual, image, inverse_here
    )
    scaled, product, part = outs[:3]
    got_e = trade(fill(outs[3:]))

    def second_coarse(
        sums_ref, table_ref, values_ref, mine_ref, image_ref, step_ref, scaled_ref, product_ref,
        first_ref, curv_ref, raw_ref, next_ref, values_out, inv_ref, quad_ref, mend_ref, work_ref
    ):
        rows = gathered(sums_ref, 2, nco, devices)
        step = step_ref[...]
        values_now = values_ref[...] - dot(dot(table_ref[...], rows), step)
        values_out[...] = values_now
        own = mine_ref[...] - dot(image_ref[...], step)
        next_ref[...] = gram_dot(scaled_ref[...], product_ref[...]) + dot(own, values_now[:nco], 0, 0)
        first, curvature = first_ref[...], curv_ref[...]
        mend_ref[...] = 2.0 * (first.T - deep_dot(raw_ref[...], step))
        inverse, good, resume = solve(0.5 * (first + first.T), identity(), work_ref, (), 4, 1)

        def keep(inverse):
            inv_ref[...] = inverse
            quad_ref[...] = deep_dot(deep_dot(inverse, curvature), inverse)

        keep(inverse)

        @pl.when(jnp.logical_not(good))
        def _():
            keep(resume())

    next_part, values, first_inverse, quad, mend = call(
        second_coarse,
        [(gram_shape, F32), ((8 * nco, cols), F32)] + [(gram_shape, F32)] * 3,
        work,
        flops=2 * 12 * unknowns * cols**2,
    )(sums, table, values, coarse_mine, coarse_image, step, scaled, product, first, curvature, raw_curvature)

    per = 8 * -(-2 * cols // (8 * devices))
    blocks_out = ((devices, per, cols), F32)

    def second_direction(*refs):
        got = take(spread(refs[:nrounds]))
        part_ref, next_ref, values_ref, deep_ref, schur_ref = refs[nrounds : nrounds + 5]
        update_ref, blocks_ref = refs[nrounds + 5 :]
        update = add_faces(part_ref[...], got) + coarse_part(deep_ref[...], values_ref[...])
        update_ref[...] = update
        high = update.astype(BF16)
        low = (update - high.astype(F32)).astype(BF16)
        both = half_dot(schur_ref[...], jnp.concatenate([high, low], axis=1))
        product = both[:, :cols] + both[:, cols:]
        square = gram_dot(update, product)
        write_blocks(blocks_ref, jnp.concatenate([next_ref[...], square], axis=0))

    update, blocks = call(second_direction, [(field, F32), blocks_out])(
        *got_e, part, next_part, values, deep_bases, schur_here
    )
    blocks = lax.all_to_all(blocks, AXES, 0, 0)

    def second_sums(blocks_ref, out_ref):
        out_ref[...] = jnp.broadcast_to(jnp.sum(blocks_ref[...], axis=0)[None], out_ref.shape)

    (sums,) = call(second_sums, [blocks_out])(blocks)
    sums = lax.all_to_all(sums, AXES, 0, 0).reshape(devices * per, cols)

    def finish(
        sums_ref, inv_ref, quad_ref, mend_ref, step_ref, dir_ref, update_ref, out_ref, work_ref
    ):
        next_gram, square = sums_ref[0:cols], sums_ref[cols : 2 * cols]
        ratio = deep_dot(inv_ref[...], next_gram)
        reduced = square - dot(next_gram, deep_dot(quad_ref[...], next_gram - mend_ref[...]), 0, 0)
        curvature = 0.5 * (reduced + reduced.T)
        step, good, resume = solve(curvature, next_gram, work_ref, (1.8, 1.8, 1.5, 1.14), 6, 2)

        def write(step):
            total = step_ref[...] + deep_dot(ratio, step)
            p, q, _ = thirds(jnp.concatenate([total, step], axis=0))
            a, b, _ = thirds(jnp.concatenate([dir_ref[...], update_ref[...]], axis=1))
            pair = plain(a, jnp.concatenate([p, q], axis=1))
            out_ref[...] = pair[:, :cols] + (pair[:, cols:] + plain(b, p))

        write(step)

        @pl.when(jnp.logical_not(good))
        def _():
            write(resume())

    (solved,) = call(finish, [(field, F32)], work)(
        sums, first_inverse, quad, mend, step, direction, update
    )
    return solved[None, None]


def solution(mesh):
    return jax.shard_map(
        local,
        mesh=mesh,
        in_specs=(
            P("gx", "gy", None, None),
            P("gx", "gy", None, None),
            P("gx", "gy", None, None),
            P("gx", "gy", None, None),
            P("gx", "gy", None, None),
            P("gx", "gy", None),
        ),
        out_specs=P("gx", "gy", None, None),
        check_vma=False,
    )
```

```python
import jax
import jax.numpy as jnp
from jax import lax
from jax.experimental import pallas as pl
from jax.experimental.pallas import tpu as pltpu
from jax.sharding import PartitionSpec as P

AXES = ("gx", "gy")
F32 = jnp.float32
BF16 = jnp.bfloat16
EXACT = lax.Precision.HIGHEST


def dot(left, right, left_dim=1, right_dim=0, precision=EXACT):
    return lax.dot_general(
        left,
        right,
        (((left_dim,), (right_dim,)), ((), ())),
        precision=precision,
        preferred_element_type=F32,
    )


def thirds(value):
    high = value.astype(BF16)
    rest = value - high.astype(F32)
    middle = rest.astype(BF16)
    return high, middle, (rest - middle.astype(F32)).astype(BF16)


def plain(left, right, left_dim=1, right_dim=0):
    return lax.dot_general(
        left, right, (((left_dim,), (right_dim,)), ((), ())), preferred_element_type=F32
    )


def deep_dot(left, right):
    a, b, c = thirds(left)
    p, q, r = thirds(right)
    return plain(
        jnp.concatenate([a, a, b, a, c, b], axis=1), jnp.concatenate([p, q, p, r, p, q], axis=0)
    )


def gram_dot(left, right):
    a, b, _ = thirds(left)
    p, q, _ = thirds(right)
    cols = right.shape[1]
    pair = plain(a, jnp.concatenate([p, q], axis=1), 0, 0)
    return pair[:, :cols] + (pair[:, cols:] + plain(b, p, 0, 0))


def flat_dot(left, right):
    a, b, _ = thirds(left)
    p, q, _ = thirds(right)
    return plain(jnp.concatenate([a, a, b], axis=1), jnp.concatenate([p, q, p], axis=0))


def half_dot(left, right):
    return lax.dot_general(
        left, right, (((1,), (0,)), ((), ())), preferred_element_type=F32
    )


def call(body, outs, scratch=(), flops=0, moved=0, far=0, copies=0, far_outs=()):
    sems = [pltpu.SemaphoreType.DMA((copies,))] if copies else []

    def run(*args):
        specs = [pl.BlockSpec(memory_space=pltpu.HBM if i < far else pltpu.VMEM) for i in range(len(args))]
        args = [pltpu.with_memory_space_constraint(a, pltpu.HBM) if i < far else a for i, a in enumerate(args)]
        results = [
            pl.BlockSpec(memory_space=pltpu.HBM if k in far_outs else pltpu.VMEM)
            for k in range(len(outs))
        ]
        return kernel_call(body, outs, scratch, flops, moved, sems, specs, results)(*args)

    return run


def kernel_call(body, outs, scratch, flops, moved, sems, specs, results):
    return pl.pallas_call(
        body,
        in_specs=specs,
        out_specs=results,
        scratch_shapes=[pltpu.VMEM(shape, kind) for shape, kind in scratch] + sems,
        out_shape=[jax.ShapeDtypeStruct(shape, kind) for shape, kind in outs],
        compiler_params=pltpu.CompilerParams(vmem_limit_bytes=48 * 1024 * 1024),
        cost_estimate=pl.CostEstimate(flops=flops, bytes_accessed=moved, transcendentals=0),
    )


def pair_rounds(size):
    first = [(i, i + 1) for i in range(0, size - 1, 2)]
    second = [(i, i + 1) for i in range(1, size - 1, 2)]
    return [pairs + [(j, i) for i, j in pairs] for pairs in (second, first)]


def exchange(sends):
    got = []
    for axis, pieces in zip(AXES, (sends[0:2], sends[2:4])):
        for pairs, piece in zip(pair_rounds(lax.axis_size(axis)), pieces):
            got.append(lax.ppermute(piece, axis, pairs) if pairs else None)
    return got


def rounds_used():
    return [bool(p) for axis in AXES for p in pair_rounds(lax.axis_size(axis))]


def even(axis):
    return lax.rem(lax.axis_index(axis), 2) == 0


def to_rounds(faces):
    ex, ey = even("gx"), even("gy")
    return [
        jnp.where(ex, faces[0], faces[1]),
        jnp.where(ex, faces[1], faces[0]),
        jnp.where(ey, faces[2], faces[3]),
        jnp.where(ey, faces[3], faces[2]),
    ]


def to_faces(parts):
    ex, ey = even("gx"), even("gy")
    b, a, d, c = parts

    def choose(flag, yes, no):
        if yes is None and no is None:
            return None
        if yes is None:
            return jnp.where(flag, jnp.zeros_like(no), no)
        if no is None:
            return jnp.where(flag, yes, jnp.zeros_like(yes))
        return jnp.where(flag, yes, no)

    return [choose(ex, b, a), choose(ex, a, b), choose(ey, d, c), choose(ey, c, d)]


def face_weights():
    ix, iy = lax.axis_index("gx"), lax.axis_index("gy")
    shared = [
        ix > 0,
        ix < lax.axis_size("gx") - 1,
        iy > 0,
        iy < lax.axis_size("gy") - 1,
    ]
    return [jnp.where(flag, 0.5, 1.0).astype(F32) for flag in shared]


def split_faces(field):
    rows = field.shape[0] // 4
    return [field[rows * f : rows * (f + 1)] for f in range(4)]


def add_faces(field, got):
    faces = [
        mine if other is None else mine + other for mine, other in zip(split_faces(field), got)
    ]
    return jnp.concatenate(faces, axis=0)


def weighted(field, weights):
    return jnp.concatenate([w * v for w, v in zip(weights, split_faces(field))], axis=0)


def write_blocks(out_ref, rows):
    per = out_ref.shape[1]
    used = rows.shape[0] // per
    if used < out_ref.shape[0]:
        out_ref[...] = jnp.zeros(out_ref.shape, F32)
    out_ref[0:used] = rows.reshape(used, per, rows.shape[1])


def solve(matrix, right, work_ref, boosts, squarings, exact):
    size = matrix.shape[0]
    row_id = lax.broadcasted_iota(jnp.int32, (size, size), 0)
    col_id = lax.broadcasted_iota(jnp.int32, (size, size), 1)
    eye = (row_id == col_id).astype(F32)
    only = matrix * eye
    by_row = lax.rsqrt(jnp.sum(only, axis=1, keepdims=True))
    by_col = lax.rsqrt(jnp.sum(only, axis=0, keepdims=True))
    unit = matrix * by_row * by_col
    bound = jnp.max(jnp.sum(jnp.abs(unit), axis=0, keepdims=True), axis=1, keepdims=True)
    scale = 1.9 / bound
    right = right * by_row
    answer = right * scale
    power = eye - scale * unit

    def step(answer, power, product=deep_dot):
        return answer + product(power, answer), product(power, power)

    for k in range(squarings):
        answer, power = step(answer, power, deep_dot if k < exact else flat_dot)
        if k < len(boosts):
            power = boosts[k] * power + (1.0 - boosts[k]) * eye
            answer = boosts[k] * answer

    def resume():
        work_ref[:, 2 * size :] = jnp.zeros((size, size), F32)

        def again(carry):
            answer, power = step(work_ref[:, 0:size], work_ref[:, size : 2 * size])
            work_ref[:, 0:size] = answer
            work_ref[:, size : 2 * size] = power
            return carry[0] + 1, jnp.max(jnp.abs(power))

        def refine(_, carry):
            work_ref[:, 0:size] = (right - deep_dot(unit, work_ref[:, 2 * size :])) * scale
            work_ref[:, size : 2 * size] = eye - scale * unit
            lax.while_loop(
                lambda carry: jnp.logical_and(carry[0] < 40, carry[1] > 1e-7),
                again,
                (jnp.int32(0), jnp.float32(1.0)),
            )
            work_ref[:, 2 * size :] = work_ref[:, 2 * size :] + work_ref[:, 0:size]
            return carry

        lax.fori_loop(0, 3, refine, jnp.int32(0))
        return work_ref[:, 2 * size :] * by_row

    good = jnp.sum(power * power) < 1e-4
    return (answer + deep_dot(power, answer)) * by_row, good, resume


def local(loads, schur, local_inverse, coarse_basis, coarse_inverse, face_map):
    loads, schur, local_inverse = loads[0, 0], schur[0, 0], local_inverse[0, 0]
    basis, coarse_rows, slot_map = coarse_basis[0, 0], coarse_inverse[0, 0], face_map[0, 0]
    unknowns, cols = loads.shape
    face = unknowns // 4
    nco, coarse_all = coarse_rows.shape
    devices = lax.axis_size("gx") * lax.axis_size("gy")
    chunks = coarse_all // cols
    used = rounds_used()
    field = (unknowns, cols)
    gram_shape = (cols, cols)
    work = [((cols, 3 * cols), F32)]
    face_out = ((face, cols), F32)

    def give(refs, faces):
        for ref, value, flag in zip(refs, to_rounds(faces), used):
            if flag:
                ref[...] = value

    def take(refs):
        return to_faces([ref[...] if flag else None for ref, flag in zip(refs, used)])

    def trade(sends):
        return [got for got in exchange(sends) if got is not None]

    def spread(refs):
        left = list(refs)
        return [left.pop(0) if flag else None for flag in used]

    nrounds = sum(used)

    def fill(values):
        left = list(values)
        return [left.pop(0) if flag else None for flag in used]

    head = face + nco + nco * chunks

    def send_loads(loads_hbm, basis_hbm, rows_hbm, map_hbm, loads_ref, basis_ref, rows_ref, map_ref, *outs):
        outs, raw_ref, sems = spread(outs[:-2]), outs[-2], outs[-1]
        fetches = [
            pltpu.make_async_copy(src, dst, sems.at[k])
            for k, (src, dst) in enumerate(
                ((loads_hbm, raw_ref), (basis_hbm, basis_ref), (rows_hbm, rows_ref), (map_hbm, map_ref))
            )
        ]
        for fetch in fetches:
            fetch.start()
        for fetch in fetches:
            fetch.wait()
        wide_loads = raw_ref[...].astype(F32)
        loads_ref[...] = wide_loads
        basis_now = basis_ref[...]
        rows_now = rows_ref[...]
        packs = []
        for f, part in enumerate(split_faces(wide_loads)):
            packs.append(
                jnp.concatenate(
                    [part, basis_now[:, face * f : face * (f + 1)]]
                    + [rows_now[:, cols * c : cols * (c + 1)] for c in range(chunks)],
                    axis=0,
                )
            )
        give(outs, packs)

    outs = call(
        send_loads,
        [(field, F32), (basis.shape, F32), (coarse_rows.shape, F32), ((1, unknowns), jnp.int32)]
        + [((head, cols), F32)] * nrounds,
        [(field, BF16)],
        far=4,
        copies=4,
    )(loads, basis, coarse_rows, slot_map.reshape(1, unknowns))
    loads, basis, coarse_rows, slot_map = outs[:4]
    got_a = trade(fill(outs[4:]))

    square = (unknowns, unknowns)

    def reorder(first_hbm, second_hbm, map_ref, first_out, second_out, first_raw, second_raw, sems):
        fetches = [
            pltpu.make_async_copy(src, dst, sems.at[k])
            for k, (src, dst) in enumerate(((first_hbm, first_raw), (second_hbm, second_raw)))
        ]
        for fetch in fetches:
            fetch.start()
        slots = lax.broadcasted_iota(jnp.int32, square, 0)
        pick = (slots == map_ref[...]).astype(F32).astype(BF16)
        for fetch, ref, out in zip(fetches, (first_raw, second_raw), (first_out, second_out)):
            fetch.wait()
            rows = half_dot(pick, ref[...]).astype(BF16)
            out[...] = plain(rows, pick, 1, 1).astype(BF16)

    inverse_here, schur_here = call(
        reorder,
        [(square, BF16)] * 2,
        [(square, BF16)] * 2,
        flops=8 * unknowns**3,
        moved=8 * unknowns**2,
        far=2,
        copies=2,
    )(local_inverse, schur, slot_map)

    def first_local(*refs):
        got = take(spread(refs[:nrounds]))
        loads_ref, inverse_ref, basis_ref = refs[nrounds : nrounds + 3]
        res_ref, scaled_ref, product_ref, part_ref, mine_ref, ci_hbm = refs[nrounds + 3 : nrounds + 9]
        sends, ci_ref, sems = spread(refs[nrounds + 9 : -2]), refs[-2], refs[-1]
        weights = face_weights()
        residual = add_faces(loads_ref[...], [g if g is None else g[:face] for g in got])
        scaled = weighted(residual, weights)
        coarse_input = dot(basis_ref[...], scaled)
        mine_ref[...] = coarse_input
        ci_ref[...] = jnp.broadcast_to(coarse_input[None], ci_ref.shape)
        copy = pltpu.make_async_copy(ci_ref, ci_hbm, sems.at[0])
        copy.start()
        product = half_dot(inverse_ref[...], scaled.astype(BF16))
        part = weighted(product, weights)
        give(sends, split_faces(part))
        res_ref[...] = residual
        scaled_ref[...] = scaled
        product_ref[...] = product
        part_ref[...] = part
        copy.wait()

    spread_rows = ((devices, nco, cols), F32)
    outs = call(
        first_local,
        [(field, F32)] * 4 + [((nco, cols), F32), spread_rows] + [face_out] * nrounds,
        [spread_rows],
        copies=1,
        far_outs=(5,),
    )(*got_a, loads, inverse_here, basis)
    residual, scaled, product, part, coarse_mine, coarse_input = outs[:6]
    got_b = trade(fill(outs[6:]))
    coarse_all_in = lax.all_to_all(coarse_input, AXES, 0, 0).reshape(coarse_all, cols)

    def first_tables(*refs):
        got = take(spread(refs[:nrounds]))
        scaled_ref, product_ref, basis_ref, rows_ref = refs[nrounds : nrounds + 4]
        gram_ref, bases_ref, deep_ref, table_ref = refs[nrounds + 4 :]
        weights = face_weights()
        gram_ref[...] = gram_dot(scaled_ref[...], product_ref[...])
        basis_now = basis_ref[...]
        bases, tables = [], []
        for f in range(4):
            mine_now = weights[f] * basis_now[:, face * f : face * (f + 1)]
            other = got[f]
            if other is None:
                both = [mine_now, jnp.zeros_like(mine_now)]
                tables += [rows_ref[...], jnp.zeros((nco, coarse_all), F32)]
            else:
                both = [mine_now, 0.5 * other[face : face + nco]]
                tables += [
                    rows_ref[...],
                    jnp.concatenate(
                        [
                            other[face + nco * (c + 1) : face + nco * (c + 2)]
                            for c in range(chunks)
                        ],
                        axis=1,
                    ),
                ]
            none = jnp.zeros((2 * nco, face), F32)
            block = jnp.concatenate(both, axis=0)
            bases.append(jnp.concatenate([block if k == f else none for k in range(4)], axis=1))
        by_row = jnp.concatenate(bases, axis=0).T
        bases_ref[...] = by_row
        a, b, c = thirds(by_row)
        deep_ref[...] = jnp.concatenate([a, a, b, a, c, b], axis=1)
        table_ref[...] = jnp.concatenate(tables, axis=0)

    gram_part, bases, deep_bases, table = call(
        first_tables,
        [
            (gram_shape, F32),
            ((unknowns, 8 * nco), F32),
            ((unknowns, 48 * nco), BF16),
            ((8 * nco, coarse_all), F32),
        ],
    )(*got_a, scaled, product, basis, coarse_rows)

    def coarse_part(deep, values):
        p, q, r = thirds(values)
        return plain(deep, jnp.concatenate([p, q, p, r, p, q], axis=0))

    mine = -(-cols // devices)
    packers = cols // mine
    tall = max(mine, nco)
    block_shape = (devices, 3, tall, cols)

    def identity():
        row_id = lax.broadcasted_iota(jnp.int32, gram_shape, 0)
        col_id = lax.broadcasted_iota(jnp.int32, gram_shape, 1)
        return (row_id == col_id).astype(F32)

    def first_coarse(all_ref, deep_ref, table_ref, mine_ref, gram_ref, values_ref, coarse_ref, first_ref):
        values = deep_dot(table_ref[...], all_ref[...])
        values_ref[...] = values
        coarse_ref[...] = coarse_part(deep_ref[...], values)
        rows, results = mine_ref[...], values[:nco]
        first_ref[...] = gram_ref[...] + dot(rows, results, 0, 0)

    values, coarse, first_part = call(
        first_coarse, [((8 * nco, cols), F32), (field, F32), (gram_shape, F32)]
    )(coarse_all_in, deep_bases, table, coarse_mine, gram_part)

    def first_direction(*refs):
        got = take(spread(refs[:nrounds]))
        part_ref, coarse_ref, bases_ref, schur_ref, first_ref = refs[nrounds : nrounds + 5]
        dir_ref, image_ref, blocks_ref = refs[nrounds + 5 : nrounds + 8]
        sends = spread(refs[nrounds + 8 :])
        if packers < devices or mine < tall:
            blocks_ref[...] = jnp.zeros(blocks_ref.shape, F32)
        else:
            blocks_ref[:, 2] = jnp.zeros((devices, tall, cols), F32)
        update = add_faces(part_ref[...], got) + coarse_ref[...]
        dir_ref[...] = update
        image = half_dot(schur_ref[...], update.astype(BF16))
        image_ref[...] = image
        give(sends, split_faces(image))
        stack = gram_dot(jnp.concatenate([update, bases_ref[...]], axis=1), image)
        curvature, shares = stack[:cols], stack[cols:]
        for at, gram in ((0, curvature), (1, first_ref[...])):
            for k in range(packers):
                blocks_ref[k, at, 0:mine] = gram[mine * k : mine * (k + 1)]
        ix, iy = lax.axis_index("gx"), lax.axis_index("gy")
        sx, sy = lax.axis_size("gx"), lax.axis_size("gy")
        own = shares[0:nco]
        for f in range(1, 4):
            own = own + shares[2 * nco * f : 2 * nco * f + nco]
        here = ix * sy + iy
        targets = [
            (here, own, None),
            (here - sy, shares[nco : 2 * nco], ix > 0),
            (here + sy, shares[3 * nco : 4 * nco], ix < sx - 1),
            (here - 1, shares[5 * nco : 6 * nco], iy > 0),
            (here + 1, shares[7 * nco : 8 * nco], iy < sy - 1),
        ]

        def put(target, rows):
            blocks_ref[target, 2, 0:nco] = rows

        for target, rows, flag in targets:
            if flag is None:
                put(target, rows)
            else:
                pl.when(flag)(lambda target=target, rows=rows: put(target, rows))

    outs = call(
        first_direction,
        [(field, F32), (field, F32), (block_shape, F32)] + [face_out] * nrounds,
    )(*got_b, part, coarse, bases, schur_here, first_part)
    direction, image, blocks = outs[:3]
    got_d = trade(fill(outs[3:]))
    blocks = lax.all_to_all(blocks, AXES, 0, 0)

    groups = 4 if devices % 4 == 0 else 1

    def first_sums(blocks_ref, sum_hbm, mine_ref, sum_ref, sems):
        total = jnp.sum(blocks_ref[...], axis=0)
        mine_ref[...] = total[2, 0:nco]
        sum_ref[...] = jnp.broadcast_to(total[None], sum_ref.shape)
        copies = [
            pltpu.make_async_copy(
                sum_ref, sum_hbm.at[pl.ds(devices // groups * k, devices // groups)], sems.at[k]
            )
            for k in range(groups)
        ]
        for copy in copies:
            copy.start()
        for copy in copies:
            copy.wait()

    sums, coarse_image = call(
        first_sums,
        [(block_shape, F32), ((nco, cols), F32)],
        [((devices // groups, 3, tall, cols), F32)],
        copies=groups,
        far_outs=(0,),
    )(blocks)
    sums = lax.all_to_all(sums, AXES, 0, 0)

    def gathered(ref, at, rows, blocks):
        return jnp.concatenate([ref[k, at, 0:rows] for k in range(blocks)], axis=0)

    def first_step(sums_ref, raw_ref, curv_ref, first_ref, step_ref, work_ref):
        raw = gathered(sums_ref, 0, mine, packers)
        curvature = 0.5 * (raw + raw.T)
        first = gathered(sums_ref, 1, mine, packers)
        raw_ref[...] = raw
        curv_ref[...] = curvature
        first_ref[...] = first
        step, good, resume = solve(curvature, first, work_ref, (1.33,), 4, 2)
        step_ref[...] = step

        @pl.when(jnp.logical_not(good))
        def _():
            step_ref[...] = resume()

    raw_curvature, curvature, first, step = call(first_step, [(gram_shape, F32)] * 4, work, flops=2 * 12 * cols**3)(
        sums
    )

    def second_local(*refs):
        got = take(spread(refs[:nrounds]))
        step_ref, res_ref, image_ref, inverse_ref = refs[nrounds : nrounds + 4]
        scaled_ref, product_ref, part_ref = refs[nrounds + 4 : nrounds + 7]
        sends = spread(refs[nrounds + 7 :])
        weights = face_weights()
        residual = res_ref[...] - dot(add_faces(image_ref[...], got), step_ref[...])
        scaled = weighted(residual, weights)
        product = half_dot(inverse_ref[...], scaled.astype(BF16))
        part = weighted(product, weights)
        part_ref[...] = part
        give(sends, split_faces(part))
        scaled_ref[...] = scaled
        product_ref[...] = product

    outs = call(second_local, [(field, F32)] * 3 + [face_out] * nrounds)(
        *got_d, step, residual, image, inverse_here
    )
    scaled, product, part = outs[:3]
    got_e = trade(fill(outs[3:]))

    def second_coarse(
        sums_ref, table_ref, values_ref, mine_ref, image_ref, step_ref, scaled_ref, product_ref,
        first_ref, curv_ref, raw_ref, part_ref, deep_ref, next_ref, partly_ref, inv_ref, quad_ref,
        mend_ref, work_ref
    ):
        rows = gathered(sums_ref, 2, nco, devices)
        step = step_ref[...]
        values_now = values_ref[...] - dot(dot(table_ref[...], rows), step)
        partly_ref[...] = part_ref[...] + coarse_part(deep_ref[...], values_now)
        own = mine_ref[...] - dot(image_ref[...], step)
        next_ref[...] = gram_dot(scaled_ref[...], product_ref[...]) + dot(own, values_now[:nco], 0, 0)
        first, curvature = first_ref[...], curv_ref[...]
        mend_ref[...] = 2.0 * (first.T - deep_dot(raw_ref[...], step))
        inverse, good, resume = solve(0.5 * (first + first.T), identity(), work_ref, (), 4, 1)

        def keep(inverse):
            inv_ref[...] = inverse
            quad_ref[...] = deep_dot(deep_dot(inverse, curvature), inverse)

        keep(inverse)

        @pl.when(jnp.logical_not(good))
        def _():
            keep(resume())

    next_part, partly, first_inverse, quad, mend = call(
        second_coarse,
        [(gram_shape, F32), (field, F32)] + [(gram_shape, F32)] * 3,
        work,
        flops=2 * 12 * unknowns * cols**2,
    )(
        sums, table, values, coarse_mine, coarse_image, step, scaled, product, first, curvature,
        raw_curvature, part, deep_bases
    )

    per = 8 * -(-2 * cols // (8 * devices))
    blocks_out = ((devices, per, cols), F32)

    def second_direction(*refs):
        got = take(spread(refs[:nrounds]))
        partly_ref, next_ref, schur_ref = refs[nrounds : nrounds + 3]
        update_ref, blocks_ref = refs[nrounds + 3 :]
        update = add_faces(partly_ref[...], got)
        update_ref[...] = update
        high = update.astype(BF16)
        low = (update - high.astype(F32)).astype(BF16)
        both = half_dot(schur_ref[...], jnp.concatenate([high, low], axis=1))
        product = both[:, :cols] + both[:, cols:]
        square = gram_dot(update, product)
        write_blocks(blocks_ref, jnp.concatenate([next_ref[...], square], axis=0))

    update, blocks = call(second_direction, [(field, F32), blocks_out])(
        *got_e, partly, next_part, schur_here
    )
    blocks = lax.all_to_all(blocks, AXES, 0, 0)

    def second_sums(blocks_ref, out_ref):
        out_ref[...] = jnp.broadcast_to(jnp.sum(blocks_ref[...], axis=0)[None], out_ref.shape)

    (sums,) = call(second_sums, [blocks_out])(blocks)
    sums = lax.all_to_all(sums, AXES, 0, 0).reshape(devices * per, cols)

    def finish(
        sums_ref, inv_ref, quad_ref, mend_ref, step_ref, dir_ref, update_ref, out_ref, work_ref
    ):
        next_gram, square = sums_ref[0:cols], sums_ref[cols : 2 * cols]
        ratio = deep_dot(inv_ref[...], next_gram)
        reduced = square - dot(next_gram, deep_dot(quad_ref[...], next_gram - mend_ref[...]), 0, 0)
        curvature = 0.5 * (reduced + reduced.T)
        step, good, resume = solve(curvature, next_gram, work_ref, (1.8, 1.8, 1.5, 1.14), 6, 2)

        def write(step):
            total = step_ref[...] + deep_dot(ratio, step)
            p, q, _ = thirds(jnp.concatenate([total, step], axis=0))
            a, b, _ = thirds(jnp.concatenate([dir_ref[...], update_ref[...]], axis=1))
            pair = plain(a, jnp.concatenate([p, q], axis=1))
            out_ref[...] = pair[:, :cols] + (pair[:, cols:] + plain(b, p))

        write(step)

        @pl.when(jnp.logical_not(good))
        def _():
            write(resume())

    (solved,) = call(finish, [(field, F32)], work)(
        sums, first_inverse, quad, mend, step, direction, update
    )
    return solved[None, None]


def solution(mesh):
    return jax.shard_map(
        local,
        mesh=mesh,
        in_specs=(
            P("gx", "gy", None, None),
            P("gx", "gy", None, None),
            P("gx", "gy", None, None),
            P("gx", "gy", None, None),
            P("gx", "gy", None, None),
            P("gx", "gy", None),
        ),
        out_specs=P("gx", "gy", None, None),
        check_vma=False,
    )
```

```python
import jax
import jax.numpy as jnp
from jax import lax
from jax.experimental import pallas as pl
from jax.experimental.pallas import tpu as pltpu
from jax.sharding import PartitionSpec as P

AXES = ("gx", "gy")
F32 = jnp.float32
BF16 = jnp.bfloat16
EXACT = lax.Precision.HIGHEST


def dot(left, right, left_dim=1, right_dim=0, precision=EXACT):
    return lax.dot_general(
        left,
        right,
        (((left_dim,), (right_dim,)), ((), ())),
        precision=precision,
        preferred_element_type=F32,
    )


def thirds(value):
    high = value.astype(BF16)
    rest = value - high.astype(F32)
    middle = rest.astype(BF16)
    return high, middle, (rest - middle.astype(F32)).astype(BF16)


def plain(left, right, left_dim=1, right_dim=0):
    return lax.dot_general(
        left, right, (((left_dim,), (right_dim,)), ((), ())), preferred_element_type=F32
    )


def deep_dot(left, right):
    a, b, c = thirds(left)
    p, q, r = thirds(right)
    cols = right.shape[1]
    pair = jnp.concatenate([p, q], axis=1)
    large = plain(jnp.concatenate([a, b], axis=1), jnp.concatenate([pair, pair], axis=0))
    small = plain(jnp.concatenate([a, c], axis=1), jnp.concatenate([r, p], axis=0))
    return large[:, :cols] + (large[:, cols:] + small)


def gram_dot(left, right):
    a, b, _ = thirds(left)
    p, q, _ = thirds(right)
    cols = right.shape[1]
    pair = plain(a, jnp.concatenate([p, q], axis=1), 0, 0)
    return pair[:, :cols] + (pair[:, cols:] + plain(b, p, 0, 0))


def flat_dot(left, right):
    a, b, _ = thirds(left)
    p, q, _ = thirds(right)
    return plain(jnp.concatenate([a, a, b], axis=1), jnp.concatenate([p, q, p], axis=0))


def half_dot(left, right):
    return lax.dot_general(
        left, right, (((1,), (0,)), ((), ())), preferred_element_type=F32
    )


def call(body, outs, scratch=(), flops=0, moved=0, far=0, copies=0, far_outs=()):
    sems = [pltpu.SemaphoreType.DMA((copies,))] if copies else []

    def run(*args):
        specs = [pl.BlockSpec(memory_space=pltpu.HBM if i < far else pltpu.VMEM) for i in range(len(args))]
        args = [pltpu.with_memory_space_constraint(a, pltpu.HBM) if i < far else a for i, a in enumerate(args)]
        results = [
            pl.BlockSpec(memory_space=pltpu.HBM if k in far_outs else pltpu.VMEM)
            for k in range(len(outs))
        ]
        return kernel_call(body, outs, scratch, flops, moved, sems, specs, results)(*args)

    return run


def kernel_call(body, outs, scratch, flops, moved, sems, specs, results):
    return pl.pallas_call(
        body,
        in_specs=specs,
        out_specs=results,
        scratch_shapes=[pltpu.VMEM(shape, kind) for shape, kind in scratch] + sems,
        out_shape=[jax.ShapeDtypeStruct(shape, kind) for shape, kind in outs],
        compiler_params=pltpu.CompilerParams(vmem_limit_bytes=48 * 1024 * 1024),
        cost_estimate=pl.CostEstimate(flops=flops, bytes_accessed=moved, transcendentals=0),
    )


def pair_rounds(size):
    first = [(i, i + 1) for i in range(0, size - 1, 2)]
    second = [(i, i + 1) for i in range(1, size - 1, 2)]
    return [pairs + [(j, i) for i, j in pairs] for pairs in (second, first)]


def exchange(sends):
    got = []
    for axis, pieces in zip(AXES, (sends[0:2], sends[2:4])):
        for pairs, piece in zip(pair_rounds(lax.axis_size(axis)), pieces):
            got.append(lax.ppermute(piece, axis, pairs) if pairs else None)
    return got


def rounds_used():
    return [bool(p) for axis in AXES for p in pair_rounds(lax.axis_size(axis))]


def even(axis):
    return lax.rem(lax.axis_index(axis), 2) == 0


def to_rounds(faces):
    ex, ey = even("gx"), even("gy")
    return [
        jnp.where(ex, faces[0], faces[1]),
        jnp.where(ex, faces[1], faces[0]),
        jnp.where(ey, faces[2], faces[3]),
        jnp.where(ey, faces[3], faces[2]),
    ]


def to_faces(parts):
    ex, ey = even("gx"), even("gy")
    b, a, d, c = parts

    def choose(flag, yes, no):
        if yes is None and no is None:
            return None
        if yes is None:
            return jnp.where(flag, jnp.zeros_like(no), no)
        if no is None:
            return jnp.where(flag, yes, jnp.zeros_like(yes))
        return jnp.where(flag, yes, no)

    return [choose(ex, b, a), choose(ex, a, b), choose(ey, d, c), choose(ey, c, d)]


def face_weights():
    ix, iy = lax.axis_index("gx"), lax.axis_index("gy")
    shared = [
        ix > 0,
        ix < lax.axis_size("gx") - 1,
        iy > 0,
        iy < lax.axis_size("gy") - 1,
    ]
    return [jnp.where(flag, 0.5, 1.0).astype(F32) for flag in shared]


def split_faces(field):
    rows = field.shape[0] // 4
    return [field[rows * f : rows * (f + 1)] for f in range(4)]


def add_faces(field, got):
    faces = [
        mine if other is None else mine + other for mine, other in zip(split_faces(field), got)
    ]
    return jnp.concatenate(faces, axis=0)


def weighted(field, weights):
    return jnp.concatenate([w * v for w, v in zip(weights, split_faces(field))], axis=0)


def write_blocks(out_ref, rows):
    per = out_ref.shape[1]
    used = rows.shape[0] // per
    if used < out_ref.shape[0]:
        out_ref[...] = jnp.zeros(out_ref.shape, F32)
    out_ref[0:used] = rows.reshape(used, per, rows.shape[1])


def solve(matrix, right, work_ref, boosts, squarings, exact):
    size = matrix.shape[0]
    row_id = lax.broadcasted_iota(jnp.int32, (size, size), 0)
    col_id = lax.broadcasted_iota(jnp.int32, (size, size), 1)
    eye = (row_id == col_id).astype(F32)
    only = matrix * eye
    by_row = lax.rsqrt(jnp.sum(only, axis=1, keepdims=True))
    by_col = lax.rsqrt(jnp.sum(only, axis=0, keepdims=True))
    unit = matrix * by_row * by_col
    bound = jnp.max(jnp.sum(jnp.abs(unit), axis=0, keepdims=True), axis=1, keepdims=True)
    scale = 1.9 / bound
    right = right * by_row
    answer = right * scale
    power = eye - scale * unit

    def step(answer, power, product=deep_dot):
        return answer + product(power, answer), product(power, power)

    for k in range(squarings):
        answer, power = step(answer, power, deep_dot if k < exact else flat_dot)
        if k < len(boosts):
            power = boosts[k] * power + (1.0 - boosts[k]) * eye
            answer = boosts[k] * answer

    def resume():
        work_ref[:, 2 * size :] = jnp.zeros((size, size), F32)

        def again(carry):
            answer, power = step(work_ref[:, 0:size], work_ref[:, size : 2 * size])
            work_ref[:, 0:size] = answer
            work_ref[:, size : 2 * size] = power
            return carry[0] + 1, jnp.max(jnp.abs(power))

        def refine(_, carry):
            work_ref[:, 0:size] = (right - deep_dot(unit, work_ref[:, 2 * size :])) * scale
            work_ref[:, size : 2 * size] = eye - scale * unit
            lax.while_loop(
                lambda carry: jnp.logical_and(carry[0] < 40, carry[1] > 1e-7),
                again,
                (jnp.int32(0), jnp.float32(1.0)),
            )
            work_ref[:, 2 * size :] = work_ref[:, 2 * size :] + work_ref[:, 0:size]
            return carry

        lax.fori_loop(0, 3, refine, jnp.int32(0))
        return work_ref[:, 2 * size :] * by_row

    good = jnp.sum(power * power) < 1e-4
    return (answer + deep_dot(power, answer)) * by_row, good, resume


def local(loads, schur, local_inverse, coarse_basis, coarse_inverse, face_map):
    loads, schur, local_inverse = loads[0, 0], schur[0, 0], local_inverse[0, 0]
    basis, coarse_rows, slot_map = coarse_basis[0, 0], coarse_inverse[0, 0], face_map[0, 0]
    unknowns, cols = loads.shape
    face = unknowns // 4
    nco, coarse_all = coarse_rows.shape
    devices = lax.axis_size("gx") * lax.axis_size("gy")
    chunks = coarse_all // cols
    used = rounds_used()
    field = (unknowns, cols)
    gram_shape = (cols, cols)
    work = [((cols, 3 * cols), F32)]
    face_out = ((face, cols), F32)

    def give(refs, faces):
        for ref, value, flag in zip(refs, to_rounds(faces), used):
            if flag:
                ref[...] = value

    def take(refs):
        return to_faces([ref[...] if flag else None for ref, flag in zip(refs, used)])

    def trade(sends):
        return [got for got in exchange(sends) if got is not None]

    def spread(refs):
        left = list(refs)
        return [left.pop(0) if flag else None for flag in used]

    nrounds = sum(used)

    def fill(values):
        left = list(values)
        return [left.pop(0) if flag else None for flag in used]

    head = face + nco + nco * chunks

    def send_loads(loads_hbm, basis_hbm, rows_hbm, map_hbm, loads_ref, basis_ref, rows_ref, map_ref, *outs):
        outs, raw_ref, sems = spread(outs[:-2]), outs[-2], outs[-1]
        fetches = [
            pltpu.make_async_copy(src, dst, sems.at[k])
            for k, (src, dst) in enumerate(
                ((loads_hbm, raw_ref), (basis_hbm, basis_ref), (rows_hbm, rows_ref), (map_hbm, map_ref))
            )
        ]
        for fetch in fetches:
            fetch.start()
        for fetch in fetches:
            fetch.wait()
        wide_loads = raw_ref[...].astype(F32)
        loads_ref[...] = wide_loads
        basis_now = basis_ref[...]
        rows_now = rows_ref[...]
        packs = []
        for f, part in enumerate(split_faces(wide_loads)):
            packs.append(
                jnp.concatenate(
                    [part, basis_now[:, face * f : face * (f + 1)]]
                    + [rows_now[:, cols * c : cols * (c + 1)] for c in range(chunks)],
                    axis=0,
                )
            )
        give(outs, packs)

    outs = call(
        send_loads,
        [(field, F32), (basis.shape, F32), (coarse_rows.shape, F32), ((1, unknowns), jnp.int32)]
        + [((head, cols), F32)] * nrounds,
        [(field, BF16)],
        far=4,
        copies=4,
    )(loads, basis, coarse_rows, slot_map.reshape(1, unknowns))
    loads, basis, coarse_rows, slot_map = outs[:4]
    got_a = trade(fill(outs[4:]))

    square = (unknowns, unknowns)

    def reorder(first_hbm, second_hbm, map_ref, first_out, second_out, first_raw, second_raw, sems):
        fetches = [
            pltpu.make_async_copy(src, dst, sems.at[k])
            for k, (src, dst) in enumerate(((first_hbm, first_raw), (second_hbm, second_raw)))
        ]
        for fetch in fetches:
            fetch.start()
        slots = lax.broadcasted_iota(jnp.int32, square, 0)
        pick = (slots == map_ref[...]).astype(F32).astype(BF16)
        for fetch, ref, out in zip(fetches, (first_raw, second_raw), (first_out, second_out)):
            fetch.wait()
            rows = half_dot(pick, ref[...]).astype(BF16)
            out[...] = plain(rows, pick, 1, 1).astype(BF16)

    inverse_here, schur_here = call(
        reorder,
        [(square, BF16)] * 2,
        [(square, BF16)] * 2,
        flops=8 * unknowns**3,
        moved=8 * unknowns**2,
        far=2,
        copies=2,
    )(local_inverse, schur, slot_map)

    def first_local(*refs):
        got = take(spread(refs[:nrounds]))
        loads_ref, inverse_ref, basis_ref = refs[nrounds : nrounds + 3]
        res_ref, scaled_ref, product_ref, part_ref, mine_ref, ci_hbm = refs[nrounds + 3 : nrounds + 9]
        sends, ci_ref, sems = spread(refs[nrounds + 9 : -2]), refs[-2], refs[-1]
        weights = face_weights()
        residual = add_faces(loads_ref[...], [g if g is None else g[:face] for g in got])
        scaled = weighted(residual, weights)
        coarse_input = dot(basis_ref[...], scaled)
        mine_ref[...] = coarse_input
        ci_ref[...] = jnp.broadcast_to(coarse_input[None], ci_ref.shape)
        copy = pltpu.make_async_copy(ci_ref, ci_hbm, sems.at[0])
        copy.start()
        product = half_dot(inverse_ref[...], scaled.astype(BF16))
        part = weighted(product, weights)
        give(sends, split_faces(part))
        res_ref[...] = residual
        scaled_ref[...] = scaled
        product_ref[...] = product
        part_ref[...] = part
        copy.wait()

    spread_rows = ((devices, nco, cols), F32)
    outs = call(
        first_local,
        [(field, F32)] * 4 + [((nco, cols), F32), spread_rows] + [face_out] * nrounds,
        [spread_rows],
        copies=1,
        far_outs=(5,),
    )(*got_a, loads, inverse_here, basis)
    residual, scaled, product, part, coarse_mine, coarse_input = outs[:6]
    got_b = trade(fill(outs[6:]))
    coarse_all_in = lax.all_to_all(coarse_input, AXES, 0, 0).reshape(coarse_all, cols)

    def first_tables(*refs):
        got = take(spread(refs[:nrounds]))
        scaled_ref, product_ref, basis_ref, rows_ref = refs[nrounds : nrounds + 4]
        gram_ref, bases_ref, deep_ref, table_ref = refs[nrounds + 4 :]
        weights = face_weights()
        gram_ref[...] = gram_dot(scaled_ref[...], product_ref[...])
        basis_now = basis_ref[...]
        bases, tables = [], []
        for f in range(4):
            mine_now = weights[f] * basis_now[:, face * f : face * (f + 1)]
            other = got[f]
            if other is None:
                both = [mine_now, jnp.zeros_like(mine_now)]
                tables += [rows_ref[...], jnp.zeros((nco, coarse_all), F32)]
            else:
                both = [mine_now, 0.5 * other[face : face + nco]]
                tables += [
                    rows_ref[...],
                    jnp.concatenate(
                        [
                            other[face + nco * (c + 1) : face + nco * (c + 2)]
                            for c in range(chunks)
                        ],
                        axis=1,
                    ),
                ]
            none = jnp.zeros((2 * nco, face), F32)
            block = jnp.concatenate(both, axis=0)
            bases.append(jnp.concatenate([block if k == f else none for k in range(4)], axis=1))
        by_row = jnp.concatenate(bases, axis=0).T
        bases_ref[...] = by_row
        a, b, c = thirds(by_row)
        deep_ref[...] = jnp.concatenate([a, a, b, a, c, b], axis=1)
        table_ref[...] = jnp.concatenate(tables, axis=0)

    gram_part, bases, deep_bases, table = call(
        first_tables,
        [
            (gram_shape, F32),
            ((unknowns, 8 * nco), F32),
            ((unknowns, 48 * nco), BF16),
            ((8 * nco, coarse_all), F32),
        ],
    )(*got_a, scaled, product, basis, coarse_rows)

    def coarse_part(deep, values):
        p, q, r = thirds(values)
        return plain(deep, jnp.concatenate([p, q, p, r, p, q], axis=0))

    mine = -(-cols // devices)
    packers = cols // mine
    tall = max(mine, nco)
    block_shape = (devices, 3, tall, cols)

    def identity():
        row_id = lax.broadcasted_iota(jnp.int32, gram_shape, 0)
        col_id = lax.broadcasted_iota(jnp.int32, gram_shape, 1)
        return (row_id == col_id).astype(F32)

    def first_coarse(all_ref, deep_ref, table_ref, mine_ref, gram_ref, values_ref, coarse_ref, first_ref):
        values = deep_dot(table_ref[...], all_ref[...])
        values_ref[...] = values
        coarse_ref[...] = coarse_part(deep_ref[...], values)
        rows, results = mine_ref[...], values[:nco]
        first_ref[...] = gram_ref[...] + dot(rows, results, 0, 0)

    values, coarse, first_part = call(
        first_coarse, [((8 * nco, cols), F32), (field, F32), (gram_shape, F32)]
    )(coarse_all_in, deep_bases, table, coarse_mine, gram_part)

    def first_direction(*refs):
        got = take(spread(refs[:nrounds]))
        part_ref, coarse_ref, bases_ref, schur_ref, first_ref = refs[nrounds : nrounds + 5]
        dir_ref, image_ref, blocks_ref = refs[nrounds + 5 : nrounds + 8]
        sends = spread(refs[nrounds + 8 :])
        if packers < devices or mine < tall:
            blocks_ref[...] = jnp.zeros(blocks_ref.shape, F32)
        else:
            blocks_ref[:, 2] = jnp.zeros((devices, tall, cols), F32)
        update = add_faces(part_ref[...], got) + coarse_ref[...]
        dir_ref[...] = update
        image = half_dot(schur_ref[...], update.astype(BF16))
        image_ref[...] = image
        give(sends, split_faces(image))
        stack = gram_dot(jnp.concatenate([update, bases_ref[...]], axis=1), image)
        curvature, shares = stack[:cols], stack[cols:]
        for at, gram in ((0, curvature), (1, first_ref[...])):
            for k in range(packers):
                blocks_ref[k, at, 0:mine] = gram[mine * k : mine * (k + 1)]
        ix, iy = lax.axis_index("gx"), lax.axis_index("gy")
        sx, sy = lax.axis_size("gx"), lax.axis_size("gy")
        own = shares[0:nco]
        for f in range(1, 4):
            own = own + shares[2 * nco * f : 2 * nco * f + nco]
        here = ix * sy + iy
        targets = [
            (here, own, None),
            (here - sy, shares[nco : 2 * nco], ix > 0),
            (here + sy, shares[3 * nco : 4 * nco], ix < sx - 1),
            (here - 1, shares[5 * nco : 6 * nco], iy > 0),
            (here + 1, shares[7 * nco : 8 * nco], iy < sy - 1),
        ]

        def put(target, rows):
            blocks_ref[target, 2, 0:nco] = rows

        for target, rows, flag in targets:
            if flag is None:
                put(target, rows)
            else:
                pl.when(flag)(lambda target=target, rows=rows: put(target, rows))

    outs = call(
        first_direction,
        [(field, F32), (field, F32), (block_shape, F32)] + [face_out] * nrounds,
    )(*got_b, part, coarse, bases, schur_here, first_part)
    direction, image, blocks = outs[:3]
    got_d = trade(fill(outs[3:]))
    blocks = lax.all_to_all(blocks, AXES, 0, 0)

    groups = 4 if devices % 4 == 0 else 1

    def first_sums(blocks_ref, sum_hbm, mine_ref, sum_ref, sems):
        total = jnp.sum(blocks_ref[...], axis=0)
        mine_ref[...] = total[2, 0:nco]
        sum_ref[...] = jnp.broadcast_to(total[None], sum_ref.shape)
        copies = [
            pltpu.make_async_copy(
                sum_ref, sum_hbm.at[pl.ds(devices // groups * k, devices // groups)], sems.at[k]
            )
            for k in range(groups)
        ]
        for copy in copies:
            copy.start()
        for copy in copies:
            copy.wait()

    sums, coarse_image = call(
        first_sums,
        [(block_shape, F32), ((nco, cols), F32)],
        [((devices // groups, 3, tall, cols), F32)],
        copies=groups,
        far_outs=(0,),
    )(blocks)
    sums = lax.all_to_all(sums, AXES, 0, 0)

    def gathered(ref, at, rows, blocks):
        return jnp.concatenate([ref[k, at, 0:rows] for k in range(blocks)], axis=0)

    def first_step(sums_ref, raw_ref, curv_ref, first_ref, step_ref, work_ref):
        raw = gathered(sums_ref, 0, mine, packers)
        curvature = 0.5 * (raw + raw.T)
        first = gathered(sums_ref, 1, mine, packers)
        raw_ref[...] = raw
        curv_ref[...] = curvature
        first_ref[...] = first
        step, good, resume = solve(curvature, first, work_ref, (1.33,), 4, 2)
        step_ref[...] = step

        @pl.when(jnp.logical_not(good))
        def _():
            step_ref[...] = resume()

    raw_curvature, curvature, first, step = call(first_step, [(gram_shape, F32)] * 4, work, flops=2 * 12 * cols**3)(
        sums
    )

    def second_local(*refs):
        got = take(spread(refs[:nrounds]))
        step_ref, res_ref, image_ref, inverse_ref = refs[nrounds : nrounds + 4]
        scaled_ref, product_ref, part_ref = refs[nrounds + 4 : nrounds + 7]
        sends = spread(refs[nrounds + 7 :])
        weights = face_weights()
        residual = res_ref[...] - deep_dot(add_faces(image_ref[...], got), step_ref[...])
        scaled = weighted(residual, weights)
        product = half_dot(inverse_ref[...], scaled.astype(BF16))
        part = weighted(product, weights)
        part_ref[...] = part
        give(sends, split_faces(part))
        scaled_ref[...] = scaled
        product_ref[...] = product

    outs = call(second_local, [(field, F32)] * 3 + [face_out] * nrounds)(
        *got_d, step, residual, image, inverse_here
    )
    scaled, product, part = outs[:3]
    got_e = trade(fill(outs[3:]))

    def second_coarse(
        sums_ref, table_ref, values_ref, mine_ref, image_ref, step_ref, scaled_ref, product_ref,
        first_ref, curv_ref, raw_ref, part_ref, deep_ref, next_ref, partly_ref, inv_ref, quad_ref,
        mend_ref, work_ref
    ):
        rows = gathered(sums_ref, 2, nco, devices)
        step = step_ref[...]
        values_now = values_ref[...] - dot(dot(table_ref[...], rows), step)
        partly_ref[...] = part_ref[...] + coarse_part(deep_ref[...], values_now)
        own = mine_ref[...] - dot(image_ref[...], step)
        next_ref[...] = gram_dot(scaled_ref[...], product_ref[...]) + dot(own, values_now[:nco], 0, 0)
        first, curvature = first_ref[...], curv_ref[...]
        mend_ref[...] = 2.0 * (first.T - deep_dot(raw_ref[...], step))
        inverse, good, resume = solve(0.5 * (first + first.T), identity(), work_ref, (), 4, 1)

        def keep(inverse):
            inv_ref[...] = inverse
            quad_ref[...] = deep_dot(deep_dot(inverse, curvature), inverse)

        keep(inverse)

        @pl.when(jnp.logical_not(good))
        def _():
            keep(resume())

    next_part, partly, first_inverse, quad, mend = call(
        second_coarse,
        [(gram_shape, F32), (field, F32)] + [(gram_shape, F32)] * 3,
        work,
        flops=2 * 12 * unknowns * cols**2,
    )(
        sums, table, values, coarse_mine, coarse_image, step, scaled, product, first, curvature,
        raw_curvature, part, deep_bases
    )

    per = 8 * -(-2 * cols // (8 * devices))
    blocks_out = ((devices, per, cols), F32)

    def second_direction(*refs):
        got = take(spread(refs[:nrounds]))
        partly_ref, next_ref, schur_ref = refs[nrounds : nrounds + 3]
        update_ref, blocks_ref = refs[nrounds + 3 :]
        update = add_faces(partly_ref[...], got)
        update_ref[...] = update
        high = update.astype(BF16)
        low = (update - high.astype(F32)).astype(BF16)
        both = half_dot(schur_ref[...], jnp.concatenate([high, low], axis=1))
        product = both[:, :cols] + both[:, cols:]
        square = gram_dot(update, product)
        write_blocks(blocks_ref, jnp.concatenate([next_ref[...], square], axis=0))

    update, blocks = call(second_direction, [(field, F32), blocks_out])(
        *got_e, partly, next_part, schur_here
    )
    blocks = lax.all_to_all(blocks, AXES, 0, 0)

    def second_sums(blocks_ref, out_ref):
        out_ref[...] = jnp.broadcast_to(jnp.sum(blocks_ref[...], axis=0)[None], out_ref.shape)

    (sums,) = call(second_sums, [blocks_out])(blocks)
    sums = lax.all_to_all(sums, AXES, 0, 0).reshape(devices * per, cols)

    def finish(
        sums_ref, inv_ref, quad_ref, mend_ref, step_ref, dir_ref, update_ref, out_ref, work_ref
    ):
        next_gram, square = sums_ref[0:cols], sums_ref[cols : 2 * cols]
        ratio = deep_dot(inv_ref[...], next_gram)
        reduced = square - dot(next_gram, deep_dot(quad_ref[...], next_gram - mend_ref[...]), 0, 0)
        curvature = 0.5 * (reduced + reduced.T)
        step, good, resume = solve(curvature, next_gram, work_ref, (1.8, 1.8, 1.5, 1.14), 6, 2)

        def write(step):
            total = step_ref[...] + deep_dot(ratio, step)
            p, q, _ = thirds(jnp.concatenate([total, step], axis=0))
            a, b, _ = thirds(jnp.concatenate([dir_ref[...], update_ref[...]], axis=1))
            pair = plain(a, jnp.concatenate([p, q], axis=1))
            out_ref[...] = pair[:, :cols] + (pair[:, cols:] + plain(b, p))

        write(step)

        @pl.when(jnp.logical_not(good))
        def _():
            write(resume())

    (solved,) = call(finish, [(field, F32)], work)(
        sums, first_inverse, quad, mend, step, direction, update
    )
    return solved[None, None]


def solution(mesh):
    return jax.shard_map(
        local,
        mesh=mesh,
        in_specs=(
            P("gx", "gy", None, None),
            P("gx", "gy", None, None),
            P("gx", "gy", None, None),
            P("gx", "gy", None, None),
            P("gx", "gy", None, None),
            P("gx", "gy", None),
        ),
        out_specs=P("gx", "gy", None, None),
        check_vma=False,
    )
```
